768 devices in a mesh: port: 24 (over x, z_hi, core), tm: 32 (over y, z_lo).
Axes of the slice: x: 4, y: 8, z: 12 (z_hi: 3, z_lo: 4; z = z_hi * 4 + z_lo), core: 2. Of those that a mesh axis runs over, the one named last changes fastest.
Arguments:
- query_rows: bfloat16 [1536, 64, 256], P('port', 'tm'), may hold values from -8 to 8
- key_rows: bfloat16 [1536, 64, 256], P('port', 'tm'), may hold values from -8 to 8
- value_rows: bfloat16 [1536, 64, 256], P('port', 'tm'), may hold values from -6 to 6
- out_grad: bfloat16 [1536, 64, 512], P('port', 'tm'), may hold values from -12 to 12
- out_weight: bfloat16 [256, 512], replicated, may hold values from -0.375 to 0.375
- adjacency: int32 [48, 48], P('port'), may hold values from 0 to 1, as said below
Outputs:
- query_grad: bfloat16 [1536, 64, 256], P('port', 'tm')
- key_grad: bfloat16 [1536, 64, 256], P('port', 'tm')
- value_grad: bfloat16 [1536, 64, 256], P('port', 'tm')
- weight_grad: float32 [256, 512], replicated
The draws below stay inside these ranges and needn't reach their ends.
Inputs may be any that keep to these rules, and one draw needn't show every extreme that they name: `adjacency`: symmetric, with ones on the diagonal.
All inputs are finite; a program needn't handle non-finite values.
Results may differ from the reference program's by a relative error of at most 0.015.
Values may be sent and summed in bfloat16 or wider, within the bound.
No kernel may reach another device: no remote copies, remote signals or barrier semaphores. Data moves between devices by JAX's collectives and lax.ppermute only.
A program may use at most 64 MiB of HBM per device.

```python
import jax
import jax.numpy as jnp
from jax import lax

DM = 512
HEADS = 4
HEAD_DIM = 64
BLK = 32
DA = 256
PORTS = 1536
HOURS = 64


def drawn_draw(key):
    shape = (PORTS, HOURS, HEADS * HEAD_DIM)
    query_key = jax.random.fold_in(key, 101)
    keys_key = jax.random.fold_in(key, 102)
    query_base = jax.random.truncated_normal(query_key, -4.0, 4.0, shape)
    key_base = jax.random.truncated_normal(keys_key, -4.0, 4.0, shape)
    return (query_base, key_base)


def draw_query_rows(key, part):
    return drawn_draw(key)[0].astype(jnp.bfloat16)


def draw_key_rows(key, part):
    return drawn_draw(key)[1].astype(jnp.bfloat16)


def draw_adjacency(key, part):
    blocks = PORTS // BLK
    picks = jax.random.randint(jax.random.fold_in(key, 7), (blocks, blocks), 0, 4)
    upper = jnp.triu((picks == 0).astype(jnp.int32), 1)
    return jnp.maximum(upper + upper.T, jnp.eye(blocks, dtype=jnp.int32))


def block_levels(rng, dims, cuts, low, top_value):
    factor_of, own = 1.0, jax.random.fold_in(rng, 6)
    for dim, parts in cuts:
        heights = jnp.exp(jax.random.uniform(jax.random.fold_in(own, dim), (parts,), jnp.float32, low / len(cuts), top_value / len(cuts)))
        factor_of = factor_of * jnp.repeat(heights, dims[dim] // parts).reshape([-1 if axis == dim else 1 for axis in range(len(dims))])
    return factor_of


def scatter_about(rng, dims, scale, bound, cuts=(), held_as=jnp.bfloat16):
    factor_of = block_levels(rng, dims, cuts, -0.22, 0.18) if cuts else 1.0
    drawn = jax.random.normal(rng, dims, jnp.float32) * scale * factor_of
    return jnp.minimum(jnp.maximum(drawn, -bound), bound).astype(held_as)


def setup_inputs(seed: int = 0) -> dict:
    seeds = jax.random.split(jax.random.key(seed), 7)
    return {
        "query_rows": draw_query_rows(jax.random.fold_in(seeds[6], 71), 0),
        "key_rows": draw_key_rows(jax.random.fold_in(seeds[6], 71), 0),
        "value_rows": scatter_about(seeds[2], (PORTS, HOURS, DA), 1.0, 6.0, ((0, 24), (1, 32))),
        "out_grad": scatter_about(seeds[3], (PORTS, HOURS, DM), 2.0, 12.0, ((0, 24), (1, 32))),
        "out_weight": scatter_about(seeds[4], (DA, DM), DA ** -0.5, 0.375),
        "adjacency": draw_adjacency(jax.random.fold_in(seeds[6], 71), 0),
    }


score_scale = 0.125


def reference(query_rows, key_rows, value_rows, out_grad, out_weight, adjacency):
    allowed = jnp.repeat(jnp.repeat(adjacency, BLK, axis=0), BLK, axis=1) == 1

    def one_hour(hour_slabs):
        q_hour, k_hour, v_hour, g_hour = hour_slabs
        out_delta = jnp.dot(g_hour, out_weight.T, preferred_element_type=jnp.float32).astype(jnp.bfloat16)
        attended_parts = []
        query_parts = []
        key_parts = []
        value_parts = []
        for head_index in range(HEADS):
            begin_col = head_index * HEAD_DIM
            end_col = begin_col + HEAD_DIM
            q_head = q_hour[:, begin_col:end_col]
            k_head = k_hour[:, begin_col:end_col]
            v_head = v_hour[:, begin_col:end_col]
            d_head = out_delta[:, begin_col:end_col]
            scores = jnp.dot(q_head, k_head.T, preferred_element_type=jnp.float32) * score_scale
            masked = jnp.where(allowed, scores, -1e30)
            row_max = jnp.max(masked, axis=1, keepdims=True)
            row_total = jnp.sum(jnp.where(allowed, jnp.exp(masked - row_max), 0.0), axis=1, keepdims=True)
            log_total = row_max + jnp.log(row_total)
            prob_rows = jnp.where(allowed, jnp.exp(masked - log_total), 0.0)
            prob_low = prob_rows.astype(jnp.bfloat16)
            attended = jnp.dot(prob_low, v_head, preferred_element_type=jnp.float32).astype(jnp.bfloat16)
            attended_parts.append(attended)
            row_term = jnp.sum(d_head.astype(jnp.float32) * attended.astype(jnp.float32), axis=1, keepdims=True)
            prob_grad = jnp.dot(d_head, v_head.T, preferred_element_type=jnp.float32)
            score_grad = (prob_rows * (prob_grad - row_term)).astype(jnp.bfloat16)
            query_parts.append(jnp.dot(score_grad, k_head, preferred_element_type=jnp.float32) * score_scale)
            key_parts.append(jnp.dot(score_grad.T, q_head, preferred_element_type=jnp.float32) * score_scale)
            value_parts.append(jnp.dot(prob_low.T, d_head, preferred_element_type=jnp.float32))
        attended_all = jnp.concatenate(attended_parts, axis=1)
        weight_term = jnp.dot(attended_all.T, g_hour, preferred_element_type=jnp.float32)
        return (jnp.concatenate(query_parts, axis=1).astype(jnp.bfloat16),
                jnp.concatenate(key_parts, axis=1).astype(jnp.bfloat16),
                jnp.concatenate(value_parts, axis=1).astype(jnp.bfloat16),
                weight_term)

    slabs = (query_rows.transpose(1, 0, 2), key_rows.transpose(1, 0, 2),
             value_rows.transpose(1, 0, 2), out_grad.transpose(1, 0, 2))
    query_grad, key_grad, value_grad, weight_terms = lax.map(one_hour, slabs)
    weight_grad = jnp.sum(weight_terms, axis=0) / HOURS
    return (query_grad.transpose(1, 0, 2), key_grad.transpose(1, 0, 2),
            value_grad.transpose(1, 0, 2), weight_grad)
```

```python
import functools

import jax
import jax.numpy as jnp
from jax import lax
from jax.experimental import pallas as pl
from jax.experimental.pallas import tpu as pltpu
from jax.sharding import Mesh, PartitionSpec as P

HEAD_DIM = 64
BLK = 32
LOG2E = 1.4426950408889634
BIG = 1e30
F32, BF16 = jnp.float32, jnp.bfloat16

PORT_AXES = ("x", "zh", "c")
TM_AXES = ("y", "zl")
NT = (((1,), (1,)), ((), ()))
NN = (((1,), (0,)), ((), ()))
TN = (((0,), (0,)), ((), ()))


def dot(a, b, dims):
    return lax.dot_general(a, b, dims, preferred_element_type=F32)


def low_half(rows):
    return lax.broadcasted_iota(jnp.int32, (rows, 128), 1) < HEAD_DIM


def swap(a):
    return jnp.concatenate([a[:, HEAD_DIM:], a[:, :HEAD_DIM]], axis=1)


def pack_kernel(parts, q_ref, k_ref, v_ref, g_ref, w_ref, adj_ref, out_ref):
    hours, ports, width = q_ref.shape
    bias = (adj_ref[...].astype(F32) - 1.0) * BIG
    low = low_half(ports)
    for h in range(hours):
        d = dot(g_ref[h], w_ref[...], NT)
        for t in range(width // 128):
            cols = slice(t * 128, (t + 1) * 128)
            q, k, v = (r[h, :, cols].astype(F32) for r in (q_ref, k_ref, v_ref))
            dd = d[:, cols]
            qs, ks, vs, ds = swap(q), swap(k), swap(v), swap(dd)
            for odd in range(2):
                n = 2 * t + odd
                top = jnp.where(low, qs, v) if odd else jnp.where(low, q, vs)
                bot = jnp.where(low, ks, dd) if odd else jnp.where(low, k, ds)
                for z in range(parts):
                    out_ref[n, z, h, :ports, :] = top.astype(BF16)
                    out_ref[n, z, h, ports : 2 * ports, :] = bot.astype(BF16)
                    out_ref[n, z, h, 2 * ports :, :] = bias.astype(BF16)


def attend_kernel(parts, rows, z_ref, r_ref, out_ref, qx, kx, dx, x1, x2, x1t, x2t, dkt, dvt):
    sources = r_ref.shape[0]
    ports = 64
    total = sources * ports
    own = total // parts
    pair = 2 * ports
    heads = own // pair
    zh = z_ref[0]
    lane = lax.broadcasted_iota(jnp.int32, (pair, 128), 1)
    row = lax.broadcasted_iota(jnp.int32, (pair, 128), 0)
    low = lane < HEAD_DIM
    for r in range(parts):
        z = lax.rem(zh + r, parts)
        for x in range(heads):
            at = r * own + x * pair
            group = x * parts + z
            src = r_ref.at[pl.ds(group * 2, 2)]
            a1 = src[:, :ports, :].reshape(pair, 128)
            a2 = src[:, ports : 2 * ports, :].reshape(pair, 128)
            m = src[:, 2 * ports : 2 * ports + 8, :].astype(F32)
            bias = jnp.concatenate(
                [jnp.broadcast_to(m[s, e : e + 1, :], (BLK, 128)) for s in range(2) for e in range(2)], axis=0
            )
            block = group * (pair // BLK) + lax.shift_right_logical(row, 5)
            hot = jnp.where(lane - HEAD_DIM == block, 1.0, 0.0)
            f1, f2 = a1.astype(F32), a2.astype(F32)
            sl = slice(at, at + pair)
            x1[sl, :] = a1
            x2[sl, :] = a2
            qx[sl, :] = jnp.where(low, f1, bias).astype(BF16)
            kx[sl, :] = jnp.where(low, f2, hot).astype(BF16)
            dx[sl, :] = jnp.where(low, 0.0, f2).astype(BF16)
            x1t[:, sl] = f1.T.astype(BF16)
            x2t[:, sl] = f2.T.astype(BF16)
    dkt[...] = jnp.zeros_like(dkt)
    dvt[...] = jnp.zeros_like(dvt)
    scale2 = 0.125 * LOG2E

    def step(at, is_own):
        s = dot(qx[pl.ds(at, rows), :], kx[...], NT)
        top = jnp.max(s, axis=1, keepdims=True)
        e = jnp.exp2((s - top) * scale2)
        inv = 1.0 / jnp.sum(e, axis=1, keepdims=True)
        p = e * inv
        p_low = p.astype(BF16)
        att = dot(p_low, x1[...], NN)
        d_rows = dx[pl.ds(at, rows), :]
        term = jnp.sum(d_rows.astype(F32) * att.astype(BF16).astype(F32), axis=1, keepdims=True)
        cols = total if is_own else own
        dp = dot(d_rows, x1[:cols, :], NT)
        ds = (p[:, :cols] * (dp - term)).astype(BF16)
        dkt[...] += dot(x1t[:, pl.ds(at, rows)], ds[:, :own], NN)
        dvt[...] += dot(x2t[:, pl.ds(at, rows)], p_low[:, :own], NN)
        if is_own:
            dq = dot(ds, x2[...], NN) * 0.125
            both = jnp.where(low_half(rows), dq, att).astype(BF16)
            for b in range(rows // ports):
                out_ref[at // ports + b, :ports, :] = both[b * ports : (b + 1) * ports, :]

    for b in range(own // rows):
        step(b * rows, True)

    def rest(b, carry):
        step(pl.multiple_of(own + b * rows, rows), False)
        return carry

    lax.fori_loop(0, (total - own) // rows, rest, 0)
    both = jnp.where(low_half(own), dkt[...].T * 0.125, dvt[...].T).astype(BF16)
    for b in range(own // ports):
        out_ref[b, ports : 2 * ports, :] = both[b * ports : (b + 1) * ports, :]


def unpack_kernel(t_ref, g_ref, q_ref, k_ref, v_ref, w_ref):
    hours, ports, width = q_ref.shape
    low = low_half(ports)
    att = []
    for h in range(hours):
        cols = []
        for t in range(width // 128):
            a = t_ref[2 * t, h, :ports, :].astype(F32)
            b = t_ref[2 * t + 1, h, :ports, :].astype(F32)
            c = t_ref[2 * t, h, ports:, :].astype(F32)
            d = t_ref[2 * t + 1, h, ports:, :].astype(F32)
            sl = slice(t * 128, (t + 1) * 128)
            q_ref[h, :, sl] = jnp.where(low, a, swap(b)).astype(BF16)
            k_ref[h, :, sl] = jnp.where(low, c, swap(d)).astype(BF16)
            v_ref[h, :, sl] = jnp.where(low, swap(c), d).astype(BF16)
            cols.append(jnp.where(low, swap(a), b))
        att.append(jnp.concatenate(cols, axis=1))
    whole = jnp.concatenate(att, axis=0).astype(BF16)
    g = g_ref[...].reshape(hours * ports, g_ref.shape[2])
    w_ref[...] = dot(whole, g, TN).astype(BF16)


def params():
    return pltpu.CompilerParams(vmem_limit_bytes=40 * 1024 * 1024)


def per_device(query_rows, key_rows, value_rows, out_grad, out_weight, adjacency):
    parts = lax.axis_size("zh")
    heads, hours = lax.axis_size("x"), lax.axis_size("c")
    port_count = lax.axis_size(PORT_AXES)
    tm_count = lax.axis_size(TM_AXES)
    ports, _, width = query_rows.shape
    q, k, v, g = (a.transpose(1, 0, 2) for a in (query_rows, key_rows, value_rows, out_grad))
    adj = jnp.pad(adjacency, ((0, 6), (HEAD_DIM, 128 - HEAD_DIM - adjacency.shape[1])))
    chunk = 2 * ports + 8
    send = pl.pallas_call(
        functools.partial(pack_kernel, parts),
        out_shape=jax.ShapeDtypeStruct((heads, parts, hours, chunk, 128), BF16),
        compiler_params=params(),
        name="pack",
    )(q, k, v, g, out_weight, adj)
    got = lax.all_to_all(send.reshape(port_count, chunk, 128), PORT_AXES, 0, 0, tiled=True)
    total = port_count * ports
    own = total // parts
    zh = lax.axis_index("zh").reshape(1)
    vec = pltpu.VMEM((total, 128), BF16)
    wide = pltpu.VMEM((128, total), BF16)
    acc = pltpu.VMEM((128, own), F32)
    back = pl.pallas_call(
        functools.partial(attend_kernel, parts, 256),
        out_shape=jax.ShapeDtypeStruct((heads * hours, 2 * ports, 128), BF16),
        in_specs=[pl.BlockSpec(memory_space=pltpu.SMEM), pl.BlockSpec(memory_space=pltpu.VMEM)],
        out_specs=pl.BlockSpec(memory_space=pltpu.VMEM),
        scratch_shapes=[vec] * 5 + [wide] * 2 + [acc] * 2,
        compiler_params=params(),
        name="attend",
    )(zh, got)
    mine = lax.all_to_all(back, ("x", "c"), 0, 0, tiled=True)
    grads = jax.ShapeDtypeStruct((hours, ports, width), BF16)
    dq, dk, dv, dw = pl.pallas_call(
        unpack_kernel,
        out_shape=(grads, grads, grads, jax.ShapeDtypeStruct((width, out_grad.shape[2]), BF16)),
        compiler_params=params(),
        name="unpack",
    )(mine.reshape(heads, hours, 2 * ports, 128), g)
    dq, dk, dv = (a.transpose(1, 0, 2) for a in (dq, dk, dv))
    rows = width // tm_count
    dw = dw.reshape(tm_count, rows, -1)
    dw = lax.all_to_all(dw, TM_AXES, 0, 0, tiled=True)
    dw = jnp.sum(dw.astype(F32), axis=0).astype(BF16)
    dw = lax.all_to_all(jnp.broadcast_to(dw, (port_count, *dw.shape)), PORT_AXES, 0, 0, tiled=True)
    dw = (jnp.sum(dw.astype(F32), axis=0) * (1.0 / (hours * tm_count))).astype(BF16)
    dw = lax.all_to_all(jnp.broadcast_to(dw, (tm_count, *dw.shape)), TM_AXES, 0, 0, tiled=True)
    return dq, dk, dv, dw.reshape(width, -1).astype(F32)


def solution(mesh):
    fine = Mesh(mesh.devices.reshape(4, 3, 2, 8, 4), PORT_AXES + TM_AXES)
    rows = P(PORT_AXES, TM_AXES, None)
    return jax.shard_map(
        per_device,
        mesh=fine,
        in_specs=(rows, rows, rows, rows, P(), P(PORT_AXES, None)),
        out_specs=(rows, rows, rows, P()),
        check_vma=False,
    )
```

```python
import functools

import jax
import jax.numpy as jnp
from jax import lax
from jax.experimental import pallas as pl
from jax.experimental.pallas import tpu as pltpu
from jax.sharding import Mesh, PartitionSpec as P

HEAD_DIM = 64
HALF = HEAD_DIM // 2
BLK = 32
LOG2E = 1.4426950408889634
BIG = 1e30
F32, BF16 = jnp.float32, jnp.bfloat16

PORT_AXES = ("x", "zh", "c")
TM_AXES = ("y", "zl")
NT = (((1,), (1,)), ((), ()))
NN = (((1,), (0,)), ((), ()))
TN = (((0,), (0,)), ((), ()))


def dot(a, b, dims):
    return lax.dot_general(a, b, dims, preferred_element_type=F32)


def low_half(rows):
    return lax.broadcasted_iota(jnp.int32, (rows, 128), 1) < HEAD_DIM


def swap(a):
    return jnp.concatenate([a[:, HEAD_DIM:], a[:, :HEAD_DIM]], axis=1)


def pack_kernel(parts, q_ref, k_ref, v_ref, g_ref, w_ref, adj_ref, out_ref):
    hours, ports, width = q_ref.shape
    bias = (adj_ref[...].astype(F32) - 1.0) * BIG
    low = low_half(ports)
    for h in range(hours):
        d = dot(g_ref[h], w_ref[...], NT)
        for t in range(width // 128):
            cols = slice(t * 128, (t + 1) * 128)
            q, k, v = (r[h, :, cols].astype(F32) for r in (q_ref, k_ref, v_ref))
            dd = d[:, cols]
            qs, ks, vs, ds = swap(q), swap(k), swap(v), swap(dd)
            for odd in range(2):
                n = 2 * t + odd
                top = jnp.where(low, qs, v) if odd else jnp.where(low, q, vs)
                bot = jnp.where(low, ks, dd) if odd else jnp.where(low, k, ds)
                for z in range(parts):
                    out_ref[n, z, h, :ports, :] = top.astype(BF16)
                    out_ref[n, z, h, ports : 2 * ports, :] = bot.astype(BF16)
                    out_ref[n, z, h, 2 * ports :, :] = bias.astype(BF16)


def attend_kernel(parts, rows, z_ref, r_ref, out_ref, qx, kx, dx, x1, x2, x1t, x2t, dkt, dvt):
    sources = r_ref.shape[0]
    ports = 64
    total = sources * ports
    own = total // parts
    pair = 2 * ports
    heads = own // pair
    zh = z_ref[0]
    lane = lax.broadcasted_iota(jnp.int32, (pair, 128), 1)
    row = lax.broadcasted_iota(jnp.int32, (pair, 128), 0)
    low = lane < HEAD_DIM
    for r in range(parts):
        z = lax.rem(zh + r, parts)
        for x in range(heads):
            at = r * own + x * pair
            group = x * parts + z
            src = r_ref.at[pl.ds(group * 2, 2)]
            a1 = src[:, :ports, :].reshape(pair, 128)
            a2 = src[:, ports : 2 * ports, :].reshape(pair, 128)
            m = src[:, 2 * ports : 2 * ports + 8, :].astype(F32)
            bias = jnp.concatenate(
                [jnp.broadcast_to(m[s, e : e + 1, :], (BLK, 128)) for s in range(2) for e in range(2)], axis=0
            )
            block = group * (pair // BLK) + lax.shift_right_logical(row, 5)
            hot = jnp.where(lane - HEAD_DIM == block, 1.0, 0.0)
            f1, f2 = a1.astype(F32), a2.astype(F32)
            sl = slice(at, at + pair)
            x1[sl, :] = a1
            x2[sl, :] = a2
            qx[sl, :] = jnp.where(low, f1, bias).astype(BF16)
            kx[sl, :] = jnp.where(low, f2, hot).astype(BF16)
            dx[sl, :] = jnp.where(low, 0.0, f2).astype(BF16)
            x1t[:, sl] = f1.T.astype(BF16)
            x2t[:, sl] = f2.T.astype(BF16)
    dkt[...] = jnp.zeros_like(dkt)
    dvt[...] = jnp.zeros_like(dvt)
    scale2 = 0.125 * LOG2E

    def step(at, is_own):
        s = dot(qx[pl.ds(at, rows), :], kx[...], NT)
        top = jnp.max(s, axis=1, keepdims=True)
        e = jnp.exp2((s - top) * scale2)
        inv = 1.0 / jnp.sum(e, axis=1, keepdims=True)
        p = e * inv
        p_low = p.astype(BF16)
        att = dot(p_low, x1[...], NN)
        d_rows = dx[pl.ds(at, rows), :]
        term = jnp.sum(d_rows.astype(F32) * att.astype(BF16).astype(F32), axis=1, keepdims=True)
        cols = total if is_own else own
        dp = dot(d_rows, x1[:cols, :], NT)
        ds = (p[:, :cols] * (dp - term)).astype(BF16)
        dkt[...] += dot(x1t[:, pl.ds(at, rows)], ds[:, :own], NN)
        dvt[...] += dot(x2t[:, pl.ds(at, rows)], p_low[:, :own], NN)
        if is_own:
            dq = dot(ds, x2[...], NN) * 0.125
            for b in range(0, rows, pair):
                one, two = att[b : b + ports], att[b + ports : b + pair]
                for c in range(2):
                    sl = slice(HEAD_DIM + c * HALF, HEAD_DIM + (c + 1) * HALF)
                    first = dq[b + c * ports : b + (c + 1) * ports, :HEAD_DIM]
                    both = jnp.concatenate([first, one[:, sl], two[:, sl]], axis=1)
                    out_ref[(at + b) // ports + c, :ports, :] = both.astype(BF16)

    for b in range(own // rows):
        step(b * rows, True)

    for b in range((total - own) // rows):
        step(own + b * rows, False)
    both = jnp.where(low_half(own), dkt[...].T * 0.125, dvt[...].T).astype(BF16)
    for b in range(own // ports):
        out_ref[b, ports : 2 * ports, :] = both[b * ports : (b + 1) * ports, :]


def unpack_kernel(t_ref, g_ref, q_ref, k_ref, v_ref, w_ref):
    hours, ports, width = q_ref.shape
    cores, model = g_ref.shape[0], g_ref.shape[3]
    heads = t_ref.shape[0]
    low = low_half(ports)
    for h in range(hours):
        for t in range(width // 128):
            a = t_ref[2 * t, h, :ports, :].astype(F32)
            b = t_ref[2 * t + 1, h, :ports, :].astype(F32)
            c = t_ref[2 * t, h, ports:, :].astype(F32)
            d = t_ref[2 * t + 1, h, ports:, :].astype(F32)
            sl = slice(t * 128, (t + 1) * 128)
            q_ref[h, :, sl] = jnp.where(low, a, swap(b)).astype(BF16)
            k_ref[h, :, sl] = jnp.where(low, c, swap(d)).astype(BF16)
            v_ref[h, :, sl] = jnp.where(low, swap(c), d).astype(BF16)
    dw = None
    for core in range(cores):
        sl = slice(HEAD_DIM + core * HALF, HEAD_DIM + (core + 1) * HALF)
        att = jnp.concatenate(
            [
                jnp.concatenate([t_ref[n, h, :ports, :].astype(F32)[:, sl] for n in range(heads)], axis=1)
                for h in range(hours)
            ],
            axis=0,
        ).astype(BF16)
        part = dot(att, g_ref[core].reshape(hours * ports, model), TN)
        dw = part if dw is None else dw + part
    dw = dw.astype(BF16)
    wide = model // 128
    for r in range(dw.shape[0] // 8):
        for c in range(wide):
            w_ref[r * wide + c] = dw[r * 8 : (r + 1) * 8, c * 128 : (c + 1) * 128]


def exchange(a, axes):
    return lax.all_to_all(a, axes, 0, 0, tiled=True)


def params():
    return pltpu.CompilerParams(vmem_limit_bytes=40 * 1024 * 1024)


def per_device(query_rows, key_rows, value_rows, out_grad, out_weight, adjacency):
    parts = lax.axis_size("zh")
    heads, hours = lax.axis_size("x"), lax.axis_size("c")
    port_count = lax.axis_size(PORT_AXES)
    tm_count = lax.axis_size(TM_AXES)
    ports, _, width = query_rows.shape
    q, k, v, g = (a.transpose(1, 0, 2) for a in (query_rows, key_rows, value_rows, out_grad))
    adj = jnp.pad(adjacency, ((0, 6), (HEAD_DIM, 128 - HEAD_DIM - adjacency.shape[1])))
    chunk = 2 * ports + 8
    send = pl.pallas_call(
        functools.partial(pack_kernel, parts),
        out_shape=jax.ShapeDtypeStruct((heads, parts, hours, chunk, 128), BF16),
        compiler_params=params(),
        name="pack",
    )(q, k, v, g, out_weight, adj)
    got = exchange(send.reshape(port_count, chunk, 128), PORT_AXES)
    total = port_count * ports
    own = total // parts
    zh = lax.axis_index("zh").reshape(1)
    vec = pltpu.VMEM((total, 128), BF16)
    wide = pltpu.VMEM((128, total), BF16)
    acc = pltpu.VMEM((128, own), F32)
    back = pl.pallas_call(
        functools.partial(attend_kernel, parts, 256),
        out_shape=jax.ShapeDtypeStruct((heads * hours, 2 * ports, 128), BF16),
        in_specs=[pl.BlockSpec(memory_space=pltpu.SMEM), pl.BlockSpec(memory_space=pltpu.VMEM)],
        out_specs=pl.BlockSpec(memory_space=pltpu.VMEM),
        scratch_shapes=[vec] * 5 + [wide] * 2 + [acc] * 2,
        compiler_params=params(),
        name="attend",
    )(zh, got)
    mine = exchange(back, ("x", "c"))
    grads = jax.ShapeDtypeStruct((hours, ports, width), BF16)
    half = heads * HALF
    wide = out_grad.shape[2] // 128
    tiles = half // 8 * wide
    dq, dk, dv, dw = pl.pallas_call(
        unpack_kernel,
        out_shape=(grads, grads, grads, jax.ShapeDtypeStruct((tiles, 8, 128), BF16)),
        compiler_params=params(),
        name="unpack",
    )(mine.reshape(heads, hours, 2 * ports, 128), lax.all_gather(g, "c"))
    dq, dk, dv = (a.transpose(1, 0, 2) for a in (dq, dk, dv))
    dw = exchange(dw, TM_AXES).reshape(tm_count, -1, 8, 128)
    dw = jnp.sum(dw.astype(F32), axis=0).astype(BF16)
    dw = exchange(jnp.broadcast_to(dw, (heads * parts, *dw.shape)), ("x", "zh"))
    dw = (jnp.sum(dw.astype(F32), axis=0) * (1.0 / (hours * tm_count))).astype(BF16)
    dw = exchange(jnp.broadcast_to(dw, (tm_count, *dw.shape)), TM_AXES)
    dw = lax.all_gather(dw, "c").reshape(2, heads, HALF // 8, wide, 8, 128)
    dw = dw.transpose(1, 0, 2, 4, 3, 5).reshape(width, -1).astype(F32)
    return dq, dk, dv, dw


def solution(mesh):
    fine = Mesh(mesh.devices.reshape(4, 3, 2, 8, 4), PORT_AXES + TM_AXES)
    rows = P(PORT_AXES, TM_AXES, None)
    return jax.shard_map(
        per_device,
        mesh=fine,
        in_specs=(rows, rows, rows, rows, P(), P(PORT_AXES, None)),
        out_specs=(rows, rows, rows, P()),
        check_vma=False,
    )
```

```python
import functools

import jax
import jax.numpy as jnp
from jax import lax
from jax.experimental import pallas as pl
from jax.experimental.pallas import tpu as pltpu
from jax.sharding import Mesh, PartitionSpec as P

HEAD_DIM = 64
BLK = 32
LANES = 128
LOG2E = 1.4426950408889634
BIG = 1e30
F32, BF16 = jnp.float32, jnp.bfloat16

PORT_AXES = ("x", "zh", "c")
TM_AXES = ("y", "zl")
NT = (((1,), (1,)), ((), ()))
NN = (((1,), (0,)), ((), ()))
TN = (((0,), (0,)), ((), ()))


def dot(a, b, dims):
    return lax.dot_general(a, b, dims, preferred_element_type=F32)


def low_half(rows):
    return lax.broadcasted_iota(jnp.int32, (rows, LANES), 1) < HEAD_DIM


def swap(a):
    return jnp.concatenate([a[:, HEAD_DIM:], a[:, :HEAD_DIM]], axis=1)


def pack_kv_kernel(k_ref, v_ref, out_ref):
    hours, ports, width = k_ref.shape
    low = low_half(ports)
    for h in range(hours):
        for t in range(width // LANES):
            cols = slice(t * LANES, (t + 1) * LANES)
            k, v = k_ref[h, :, cols].astype(F32), v_ref[h, :, cols].astype(F32)
            out_ref[2 * t, h] = jnp.where(low, k, swap(v)).astype(BF16)
            out_ref[2 * t + 1, h] = jnp.where(low, swap(k), v).astype(BF16)


def pack_qg_kernel(q_ref, g_ref, adj_ref, out_ref):
    hours, ports, width = q_ref.shape
    low = low_half(ports)
    bias = (adj_ref[...].astype(F32) - 1.0) * BIG
    bias = jnp.concatenate(
        [jnp.broadcast_to(bias[b : b + 1, :], (BLK, LANES)) for b in range(ports // BLK)], axis=0
    )
    for h in range(hours):
        for t in range(width // LANES):
            q = q_ref[h, :, t * LANES : (t + 1) * LANES].astype(F32)
            out_ref[2 * t, h, :, :LANES] = jnp.where(low, q, bias).astype(BF16)
            out_ref[2 * t + 1, h, :, :LANES] = jnp.where(low, swap(q), bias).astype(BF16)
        for n in range(out_ref.shape[0]):
            out_ref[n, h, :, LANES:] = g_ref[h]


def attend_kernel(
    rows, z_ref, kv0_ref, kv1_ref, kv2_ref, qg_ref, w_ref, d0_ref, d1_ref, d2_ref, dq_ref, dw_ref, kx, kv, dkt, dvt
):
    group, ports, _ = kv0_ref.shape
    own = group * ports
    total = 3 * own
    lane = lax.broadcasted_iota(jnp.int32, (own, LANES), 1)
    row = lax.broadcasted_iota(jnp.int32, (own, LANES), 0)
    for r, ref in enumerate((kv0_ref, kv1_ref, kv2_ref)):
        z = lax.rem(z_ref[0] + r, 3)
        part = ref[...].reshape(own, LANES)
        pair = lax.shift_right_logical(row, 7)
        block = (pair * 3 + z) * 4 + lax.bitwise_and(lax.shift_right_logical(row, 5), 3)
        hot = jnp.where(lane - HEAD_DIM == block, 1.0, 0.0)
        sl = slice(r * own, (r + 1) * own)
        kv[sl, :] = part
        kx[sl, :] = jnp.where(lane < HEAD_DIM, part.astype(F32), hot).astype(BF16)
    w_n = jnp.concatenate([jnp.zeros_like(w_ref), w_ref[...]], axis=0)
    scale2 = 0.125 * LOG2E
    low = low_half(rows)
    per = rows // ports
    dw = None
    for b in range(own // rows):
        mine = qg_ref[b * per : (b + 1) * per]
        qx = mine[:, :, :LANES].reshape(rows, LANES)
        g = mine[:, :, LANES:].reshape(rows, -1)
        d = dot(g, w_n, NT).astype(BF16)
        s = dot(qx, kx[...], NT)
        top = jnp.max(s, axis=1, keepdims=True)
        e = jnp.exp2((s - top) * scale2)
        p = e * (1.0 / jnp.sum(e, axis=1, keepdims=True))
        p_low = p.astype(BF16)
        att = dot(p_low, kv[...], NN).astype(BF16)
        part = dot(att, g, TN)
        dw = part if dw is None else dw + part
        d32 = d.astype(F32)
        term = jnp.sum(d32 * att.astype(F32), axis=1, keepdims=True)
        dp = dot(d, kv[...], NT)
        ds = (p * (dp - term)).astype(BF16)
        dq = dot(ds, kv[...], NN) * 0.125
        qdt = jnp.where(low, qx.astype(F32), d32).T.astype(BF16)
        dk_part = dot(qdt[:HEAD_DIM], ds, NN)
        dv_part = dot(qdt[HEAD_DIM:], p_low, NN)
        if b:
            dkt[...] += dk_part
            dvt[...] += dv_part
        else:
            dkt[...] = dk_part
            dvt[...] = dv_part
        half = ports // 2
        for i in range(per):
            a, c = dq[i * ports : i * ports + half], dq[i * ports + half : (i + 1) * ports]
            dq_ref[b * per + i] = jnp.where(low_half(half), a, swap(c)).astype(BF16)
    dw = dw[HEAD_DIM:].astype(BF16)
    wide = dw.shape[1] // LANES
    for r in range(HEAD_DIM // 8):
        for c in range(wide):
            dw_ref[r * wide + c] = dw[r * 8 : (r + 1) * 8, c * LANES : (c + 1) * LANES]
    for r, ref in enumerate((d0_ref, d1_ref, d2_ref)):
        sl = slice(r * own, (r + 1) * own)
        both = jnp.concatenate([dkt[:, sl] * 0.125, dvt[:, sl]], axis=0).T
        ref[...] = both.astype(ref.dtype).reshape(ref.shape)


def merge_kernel(d0_ref, d1_ref, d2_ref, dq_ref, out_ref):
    ports = d0_ref.shape[1]
    summed = d0_ref[...] + d1_ref[...].astype(F32) + d2_ref[...].astype(F32)
    out_ref[:, :ports, :] = summed.astype(BF16)
    out_ref[:, ports:, :] = dq_ref[...]


def unpack_kernel(t_ref, q_ref, k_ref, v_ref):
    hours, ports, width = q_ref.shape
    low = low_half(ports)
    half = ports // 2
    lh = low_half(half)
    for h in range(hours):
        for t in range(width // LANES):
            sl = slice(t * LANES, (t + 1) * LANES)
            c, d = (t_ref[n, h, :ports].astype(F32) for n in (2 * t, 2 * t + 1))
            k_ref[h, :, sl] = jnp.where(low, c, swap(d)).astype(BF16)
            v_ref[h, :, sl] = jnp.where(low, swap(c), d).astype(BF16)
            a, b = (t_ref[n, h, ports:].astype(F32) for n in (2 * t, 2 * t + 1))
            q_ref[h, :half, sl] = jnp.where(lh, a, swap(b)).astype(BF16)
            q_ref[h, half:, sl] = jnp.where(lh, swap(a), b).astype(BF16)


def call(kernel, outs, *args, scratch=(), name):
    return pl.pallas_call(
        kernel,
        out_shape=outs,
        scratch_shapes=scratch,
        compiler_params=pltpu.CompilerParams(vmem_limit_bytes=40 * 1024 * 1024),
        name=name,
    )(*args)


def shape(*dims):
    return jax.ShapeDtypeStruct(dims, BF16)


def exchange(a, axes):
    return lax.all_to_all(a, axes, 0, 0, tiled=True)


def shift(a, by):
    return lax.ppermute(a, "zh", [((i + by) % 3, i) for i in range(3)])


def per_device(query_rows, key_rows, value_rows, out_grad, out_weight, adjacency):
    parts = lax.axis_size("zh")
    heads, hours = lax.axis_size("x"), lax.axis_size("c")
    port_count = lax.axis_size(PORT_AXES)
    tm_count = lax.axis_size(TM_AXES)
    ports, _, width = query_rows.shape
    model = out_grad.shape[2]
    group = heads * hours
    total = port_count * ports
    q, k, v, g = (a.transpose(1, 0, 2) for a in (query_rows, key_rows, value_rows, out_grad))
    kv_send = call(pack_kv_kernel, shape(heads, hours, ports, LANES), k, v, name="pack_kv")
    kv0 = exchange(kv_send.reshape(group, ports, LANES), ("x", "c"))
    adj = jnp.pad(adjacency, ((0, 0), (HEAD_DIM, LANES - HEAD_DIM - adjacency.shape[1])))
    qg_send = call(pack_qg_kernel, shape(heads, hours, ports, LANES + model), q, g, adj, name="pack_qg")
    kv0, qg_send = lax.optimization_barrier((kv0, qg_send))
    kv1, kv2 = shift(kv0, 1), shift(kv0, 2)
    qg_got = exchange(qg_send.reshape(group, ports, LANES + model), ("x", "c"))
    w_n = lax.dynamic_slice_in_dim(out_weight, lax.axis_index("x") * HEAD_DIM, HEAD_DIM, 0)
    tiles = HEAD_DIM * model // (8 * LANES)
    vec, acc = pltpu.VMEM((total, LANES), BF16), pltpu.VMEM((HEAD_DIM, total), F32)
    block = shape(group, ports, LANES)
    vmem = pl.BlockSpec(memory_space=pltpu.VMEM)
    d0, d1, d2, dq, dw = pl.pallas_call(
        functools.partial(attend_kernel, 256),
        out_shape=(
            jax.ShapeDtypeStruct(block.shape, F32),
            block,
            block,
            shape(group, ports // 2, LANES),
            shape(tiles, 8, LANES),
        ),
        in_specs=[pl.BlockSpec(memory_space=pltpu.SMEM)] + [vmem] * 5,
        out_specs=(vmem,) * 5,
        scratch_shapes=[vec, vec, acc, acc],
        compiler_params=pltpu.CompilerParams(vmem_limit_bytes=40 * 1024 * 1024),
        name="attend",
    )(lax.axis_index("zh").reshape(1), kv0, kv1, kv2, qg_got, w_n)
    d1, d2 = shift(d1, 2), shift(d2, 1)
    dw = exchange(dw, TM_AXES)
    dw = jnp.sum(dw.reshape(tm_count, -1, 8, LANES).astype(F32), axis=0).astype(BF16)
    dw = exchange(jnp.broadcast_to(dw, (port_count, *dw.shape)), PORT_AXES)
    back = call(merge_kernel, shape(group, ports + ports // 2, LANES), d0, d1, d2, dq, name="merge")
    back = exchange(back, ("x", "c"))
    dw = dw.reshape(heads, parts, hours, -1, 8, LANES).astype(F32)
    dw = (jnp.sum(dw, axis=(1, 2)) * (1.0 / (hours * tm_count))).astype(BF16)
    dw = exchange(jnp.broadcast_to(dw, (tm_count, *dw.shape)), TM_AXES)
    dw = dw.transpose(1, 0, 2, 3, 4).reshape(heads, HEAD_DIM // 8, model // LANES, 8, LANES)
    dw = dw.transpose(0, 1, 3, 2, 4).reshape(width, model).astype(F32)
    grads = shape(hours, ports, width)
    grads = call(
        unpack_kernel, (grads,) * 3, back.reshape(heads, hours, ports + ports // 2, LANES), name="unpack"
    )
    return *(a.transpose(1, 0, 2) for a in grads), dw


def solution(mesh):
    fine = Mesh(mesh.devices.reshape(4, 3, 2, 8, 4), PORT_AXES + TM_AXES)
    rows = P(PORT_AXES, TM_AXES, None)
    return jax.shard_map(
        per_device,
        mesh=fine,
        in_specs=(rows, rows, rows, rows, P(), P(PORT_AXES, None)),
        out_specs=(rows, rows, rows, P()),
        check_vma=False,
    )
```

```python
import functools

import jax
import jax.numpy as jnp
from jax import lax
from jax.experimental import pallas as pl
from jax.experimental.pallas import tpu as pltpu
from jax.sharding import Mesh, PartitionSpec as P

HEAD_DIM = 64
BLK = 32
LANES = 128
LOG2E = 1.4426950408889634
BIG = 1e30
F32, BF16 = jnp.float32, jnp.bfloat16

PORT_AXES = ("x", "zh", "c")
TM_AXES = ("y", "zl")
NT = (((1,), (1,)), ((), ()))
NN = (((1,), (0,)), ((), ()))
TN = (((0,), (0,)), ((), ()))


def dot(a, b, dims):
    return lax.dot_general(a, b, dims, preferred_element_type=F32)


def low_half(rows):
    return lax.broadcasted_iota(jnp.int32, (rows, LANES), 1) < HEAD_DIM


def swap(a):
    return jnp.concatenate([a[:, HEAD_DIM:], a[:, :HEAD_DIM]], axis=1)


def pack_kv_kernel(k_ref, v_ref, out_ref):
    hours, ports, width = k_ref.shape
    low = low_half(ports)
    for h in range(hours):
        for t in range(width // LANES):
            cols = slice(t * LANES, (t + 1) * LANES)
            k, v = k_ref[h, :, cols].astype(F32), v_ref[h, :, cols].astype(F32)
            out_ref[2 * t, h] = jnp.where(low, k, swap(v)).astype(BF16)
            out_ref[2 * t + 1, h] = jnp.where(low, swap(k), v).astype(BF16)


def pack_qg_kernel(q_ref, g_ref, adj_ref, out_ref):
    hours, ports, width = q_ref.shape
    low = low_half(ports)
    bias = (adj_ref[...].astype(F32) - 1.0) * BIG
    bias = jnp.concatenate(
        [jnp.broadcast_to(bias[b : b + 1, :], (BLK, LANES)) for b in range(ports // BLK)], axis=0
    )
    for h in range(hours):
        for t in range(width // LANES):
            q = q_ref[h, :, t * LANES : (t + 1) * LANES].astype(F32)
            out_ref[2 * t, h, :, :LANES] = jnp.where(low, q, bias).astype(BF16)
            out_ref[2 * t + 1, h, :, :LANES] = jnp.where(low, swap(q), bias).astype(BF16)
        for n in range(out_ref.shape[0]):
            out_ref[n, h, :, LANES:] = g_ref[h]


def attend_kernel(
    rows, z_ref, kv0_ref, kv1_ref, kv2_ref, qg_ref, w_ref, d0_ref, d1_ref, d2_ref, dq_ref, dw_ref, kx, kv, dkt, dvt
):
    group, ports, _ = kv0_ref.shape
    own = group * ports
    total = 3 * own
    lane = lax.broadcasted_iota(jnp.int32, (own, LANES), 1)
    row = lax.broadcasted_iota(jnp.int32, (own, LANES), 0)
    for r, ref in enumerate((kv0_ref, kv1_ref, kv2_ref)):
        z = lax.rem(z_ref[0] + r, 3)
        part = ref[...].reshape(own, LANES)
        pair = lax.shift_right_logical(row, 7)
        block = (pair * 3 + z) * 4 + lax.bitwise_and(lax.shift_right_logical(row, 5), 3)
        hot = jnp.where(lane - HEAD_DIM == block, 1.0, 0.0)
        sl = slice(r * own, (r + 1) * own)
        kv[sl, :] = part
        kx[sl, :] = jnp.where(lane < HEAD_DIM, part.astype(F32), hot).astype(BF16)
    w_n = jnp.concatenate([jnp.zeros_like(w_ref), w_ref[...]], axis=0)
    scale2 = 0.125 * LOG2E
    low = low_half(rows)
    per = rows // ports
    dw = None
    for b in range(own // rows):
        mine = qg_ref[b * per : (b + 1) * per]
        qx = mine[:, :, :LANES].reshape(rows, LANES)
        g = mine[:, :, LANES:].reshape(rows, -1)
        d = dot(g, w_n, NT).astype(BF16)
        s = dot(qx, kx[...], NT)
        top = jnp.max(s, axis=1, keepdims=True)
        e = jnp.exp2((s - top) * scale2)
        p = e * (1.0 / jnp.sum(e, axis=1, keepdims=True))
        p_low = p.astype(BF16)
        att = dot(p_low, kv[...], NN).astype(BF16)
        part = dot(att, g, TN)
        dw = part if dw is None else dw + part
        d32 = d.astype(F32)
        term = jnp.sum(d32 * att.astype(F32), axis=1, keepdims=True)
        dp = dot(d, kv[...], NT)
        ds = (p * (dp - term)).astype(BF16)
        dq = dot(ds, kv[...], NN) * 0.125
        qdt = jnp.where(low, qx.astype(F32), d32).T.astype(BF16)
        dk_part = dot(qdt[:HEAD_DIM], ds, NN)
        dv_part = dot(qdt[HEAD_DIM:], p_low, NN)
        if b:
            dkt[...] += dk_part
            dvt[...] += dv_part
        else:
            dkt[...] = dk_part
            dvt[...] = dv_part
        half = ports // 2
        for i in range(per):
            a, c = dq[i * ports : i * ports + half], dq[i * ports + half : (i + 1) * ports]
            dq_ref[b * per + i] = jnp.where(low_half(half), a, swap(c)).astype(BF16)
    dw = dw[HEAD_DIM:].astype(BF16)
    wide = dw.shape[1] // LANES
    for r in range(HEAD_DIM // 8):
        for c in range(wide):
            dw_ref[r * wide + c] = dw[r * 8 : (r + 1) * 8, c * LANES : (c + 1) * LANES]
    for r, ref in enumerate((d0_ref, d1_ref, d2_ref)):
        sl = slice(r * own, (r + 1) * own)
        both = jnp.concatenate([dkt[:, sl] * 0.125, dvt[:, sl]], axis=0).T
        ref[...] = both.astype(ref.dtype).reshape(ref.shape)


def merge_kernel(d0_ref, d1_ref, d2_ref, dq_ref, out_ref):
    ports = d0_ref.shape[1]
    summed = d0_ref[...] + d1_ref[...].astype(F32) + d2_ref[...].astype(F32)
    out_ref[:, :ports, :] = summed.astype(BF16)
    out_ref[:, ports:, :] = dq_ref[...]


def unpack_kernel(t_ref, q_ref, k_ref, v_ref):
    hours, ports, width = q_ref.shape
    low = low_half(ports)
    half = ports // 2
    lh = low_half(half)
    for h in range(hours):
        for t in range(width // LANES):
            sl = slice(t * LANES, (t + 1) * LANES)
            c, d = (t_ref[n, h, :ports].astype(F32) for n in (2 * t, 2 * t + 1))
            k_ref[h, :, sl] = jnp.where(low, c, swap(d)).astype(BF16)
            v_ref[h, :, sl] = jnp.where(low, swap(c), d).astype(BF16)
            a, b = (t_ref[n, h, ports:].astype(F32) for n in (2 * t, 2 * t + 1))
            q_ref[h, :half, sl] = jnp.where(lh, a, swap(b)).astype(BF16)
            q_ref[h, half:, sl] = jnp.where(lh, swap(a), b).astype(BF16)


def call(kernel, outs, *args, scratch=(), name):
    return pl.pallas_call(
        kernel,
        out_shape=outs,
        scratch_shapes=scratch,
        compiler_params=pltpu.CompilerParams(vmem_limit_bytes=40 * 1024 * 1024),
        name=name,
    )(*args)


def shape(*dims):
    return jax.ShapeDtypeStruct(dims, BF16)


def exchange(a, axes):
    return lax.all_to_all(a, axes, 0, 0, tiled=True)


def shift(a, by):
    return lax.ppermute(a, "zh", [((i + by) % 3, i) for i in range(3)])


def per_device(query_rows, key_rows, value_rows, out_grad, out_weight, adjacency):
    parts = lax.axis_size("zh")
    heads, hours = lax.axis_size("x"), lax.axis_size("c")
    port_count = lax.axis_size(PORT_AXES)
    tm_count = lax.axis_size(TM_AXES)
    ports, _, width = query_rows.shape
    model = out_grad.shape[2]
    group = heads * hours
    total = port_count * ports
    q, k, v, g = (a.transpose(1, 0, 2) for a in (query_rows, key_rows, value_rows, out_grad))
    kv_send = call(pack_kv_kernel, shape(heads, hours, ports, LANES), k, v, name="pack_kv")
    kv0 = exchange(kv_send.reshape(group, ports, LANES), ("x", "c"))
    adj = jnp.pad(adjacency, ((0, 0), (HEAD_DIM, LANES - HEAD_DIM - adjacency.shape[1])))
    qg_send = call(pack_qg_kernel, shape(heads, hours, ports, LANES + model), q, g, adj, name="pack_qg")
    kv0, qg_send = lax.optimization_barrier((kv0, qg_send))
    kv1, kv2 = shift(kv0, 1), shift(kv0, 2)
    qg_got = exchange(qg_send.reshape(group, ports, LANES + model), ("x", "c"))
    w_n = lax.dynamic_slice_in_dim(out_weight, lax.axis_index("x") * HEAD_DIM, HEAD_DIM, 0)
    tiles = HEAD_DIM * model // (8 * LANES)
    vec, acc = pltpu.VMEM((total, LANES), BF16), pltpu.VMEM((HEAD_DIM, total), F32)
    block = shape(group, ports, LANES)
    vmem = pl.BlockSpec(memory_space=pltpu.VMEM)
    d0, d1, d2, dq, dw = pl.pallas_call(
        functools.partial(attend_kernel, 256),
        out_shape=(
            jax.ShapeDtypeStruct(block.shape, F32),
            block,
            block,
            shape(group, ports // 2, LANES),
            shape(tiles, 8, LANES),
        ),
        in_specs=[pl.BlockSpec(memory_space=pltpu.SMEM)] + [vmem] * 5,
        out_specs=(vmem,) * 5,
        scratch_shapes=[vec, vec, acc, acc],
        compiler_params=pltpu.CompilerParams(vmem_limit_bytes=40 * 1024 * 1024),
        name="attend",
    )(lax.axis_index("zh").reshape(1), kv0, kv1, kv2, qg_got, w_n)
    d1, d2 = shift(d1, 2), shift(d2, 1)
    dw = exchange(dw, TM_AXES)
    dw, d1, d2 = lax.optimization_barrier((dw, d1, d2))
    dw = jnp.sum(dw.reshape(tm_count, -1, 8, LANES).astype(F32), axis=0).astype(BF16)
    dw = exchange(jnp.broadcast_to(dw, (port_count, *dw.shape)), PORT_AXES)
    back = call(merge_kernel, shape(group, ports + ports // 2, LANES), d0, d1, d2, dq, name="merge")
    back = exchange(back, ("x", "c"))
    dw = dw.reshape(heads, parts, hours, -1, 8, LANES).astype(F32)
    dw = (jnp.sum(dw, axis=(1, 2)) * (1.0 / (hours * tm_count))).astype(BF16)
    dw = exchange(jnp.broadcast_to(dw, (tm_count, *dw.shape)), TM_AXES)
    dw = dw.transpose(1, 0, 2, 3, 4).reshape(heads, HEAD_DIM // 8, model // LANES, 8, LANES)
    dw = dw.transpose(0, 1, 3, 2, 4).reshape(width, model).astype(F32)
    grads = shape(hours, ports, width)
    grads = call(
        unpack_kernel, (grads,) * 3, back.reshape(heads, hours, ports + ports // 2, LANES), name="unpack"
    )
    return *(a.transpose(1, 0, 2) for a in grads), dw


def solution(mesh):
    fine = Mesh(mesh.devices.reshape(4, 3, 2, 8, 4), PORT_AXES + TM_AXES)
    rows = P(PORT_AXES, TM_AXES, None)
    return jax.shard_map(
        per_device,
        mesh=fine,
        in_specs=(rows, rows, rows, rows, P(), P(PORT_AXES, None)),
        out_specs=(rows, rows, rows, P()),
        check_vma=False,
    )
```

```python
import functools

import jax
import jax.numpy as jnp
from jax import lax
from jax.experimental import pallas as pl
from jax.experimental.pallas import tpu as pltpu
from jax.sharding import Mesh, PartitionSpec as P

HEAD_DIM = 64
BLK = 32
LANES = 128
LOG2E = 1.4426950408889634
BIG = 1e30
F32, BF16 = jnp.float32, jnp.bfloat16

PORT_AXES = ("x", "zh", "c")
TM_AXES = ("y", "zl")
NT = (((1,), (1,)), ((), ()))
NN = (((1,), (0,)), ((), ()))
TN = (((0,), (0,)), ((), ()))


def dot(a, b, dims):
    return lax.dot_general(a, b, dims, preferred_element_type=F32)


def low_half(rows):
    return lax.broadcasted_iota(jnp.int32, (rows, LANES), 1) < HEAD_DIM


def swap(a):
    return jnp.concatenate([a[:, HEAD_DIM:], a[:, :HEAD_DIM]], axis=1)


def pack_kv_kernel(k_ref, v_ref, out_ref):
    hours, ports, width = k_ref.shape
    low = low_half(ports)
    for h in range(hours):
        for t in range(width // LANES):
            cols = slice(t * LANES, (t + 1) * LANES)
            k, v = k_ref[h, :, cols].astype(F32), v_ref[h, :, cols].astype(F32)
            out_ref[2 * t, h] = jnp.where(low, k, swap(v)).astype(BF16)
            out_ref[2 * t + 1, h] = jnp.where(low, swap(k), v).astype(BF16)


def pack_qg_kernel(q_ref, g_ref, adj_ref, out_ref):
    hours, ports, width = q_ref.shape
    low = low_half(ports)
    bias = (adj_ref[...].astype(F32) - 1.0) * BIG
    bias = jnp.concatenate(
        [jnp.broadcast_to(bias[b : b + 1, :], (BLK, LANES)) for b in range(ports // BLK)], axis=0
    )
    for h in range(hours):
        for t in range(width // LANES):
            q = q_ref[h, :, t * LANES : (t + 1) * LANES].astype(F32)
            out_ref[2 * t, h, :, :LANES] = jnp.where(low, q, bias).astype(BF16)
            out_ref[2 * t + 1, h, :, :LANES] = jnp.where(low, swap(q), bias).astype(BF16)
        for n in range(out_ref.shape[0]):
            out_ref[n, h, :, LANES:] = g_ref[h]


def attend_kernel(rows, kv_ref, qg_ref, w_ref, out_ref, dw_ref, kx, kv, dkt, dvt):
    parts, group, ports, _ = kv_ref.shape
    own = group * ports
    total = parts * own
    lane = lax.broadcasted_iota(jnp.int32, (own, LANES), 1)
    row = lax.broadcasted_iota(jnp.int32, (own, LANES), 0)
    pair = lax.shift_right_logical(row, 7)
    inner = lax.bitwise_and(lax.shift_right_logical(row, 5), 3)
    for z in range(parts):
        part = kv_ref[z].reshape(own, LANES)
        hot = jnp.where(lane - HEAD_DIM == (pair * parts + z) * 4 + inner, 1.0, 0.0)
        sl = slice(z * own, (z + 1) * own)
        kv[sl, :] = part
        kx[sl, :] = jnp.where(lane < HEAD_DIM, part.astype(F32), hot).astype(BF16)
    w_n = jnp.concatenate([jnp.zeros_like(w_ref), w_ref[...]], axis=0)
    scale2 = 0.125 * LOG2E
    low = low_half(rows)
    per = rows // ports
    dw = None
    for b in range(own // rows):
        mine = qg_ref[b * per : (b + 1) * per]
        qx = mine[:, :, :LANES].reshape(rows, LANES)
        g = mine[:, :, LANES:].reshape(rows, -1)
        d = dot(g, w_n, NT).astype(BF16)
        s = dot(qx, kx[...], NT)
        top = jnp.max(s, axis=1, keepdims=True)
        e = jnp.exp2((s - top) * scale2)
        p = e * (1.0 / jnp.sum(e, axis=1, keepdims=True))
        p_low = p.astype(BF16)
        att = dot(p_low, kv[...], NN).astype(BF16)
        part = dot(att, g, TN)
        dw = part if dw is None else dw + part
        d32 = d.astype(F32)
        term = jnp.sum(d32 * att.astype(F32), axis=1, keepdims=True)
        dp = dot(d, kv[...], NT)
        ds = (p * (dp - term)).astype(BF16)
        dq = dot(ds, kv[...], NN) * 0.125
        qdt = jnp.where(low, qx.astype(F32), d32).T.astype(BF16)
        dk_part = dot(qdt[:HEAD_DIM], ds, NN)
        dv_part = dot(qdt[HEAD_DIM:], p_low, NN)
        if b:
            dkt[...] += dk_part
            dvt[...] += dv_part
        else:
            dkt[...] = dk_part
            dvt[...] = dv_part
        half = ports // 2
        for i in range(per):
            a, c = dq[i * ports : i * ports + half], dq[i * ports + half : (i + 1) * ports]
            both = jnp.where(low_half(half), a, swap(c)).astype(BF16)
            for z in range(parts):
                out_ref[(b * per + i) // 2, z, i % 2, ports : ports + half, :] = both
    dw = dw[HEAD_DIM:].astype(BF16)
    wide = dw.shape[1] // LANES
    for r in range(HEAD_DIM // 8):
        for c in range(wide):
            dw_ref[r * wide + c] = dw[r * 8 : (r + 1) * 8, c * LANES : (c + 1) * LANES]
    for z in range(parts):
        sl = slice(z * own, (z + 1) * own)
        both = jnp.concatenate([dkt[:, sl] * 0.125, dvt[:, sl]], axis=0).T.astype(BF16)
        for i in range(group):
            out_ref[i // 2, z, i % 2, :ports, :] = both[i * ports : (i + 1) * ports]
            out_ref[i // 2, z, i % 2, ports + half :, :] = jnp.zeros((8, LANES), BF16)


def unpack_kernel(z_ref, t_ref, q_ref, k_ref, v_ref):
    hours, ports, width = q_ref.shape
    low = low_half(ports)
    half = ports // 2
    lh = low_half(half)
    z_own = z_ref[0]
    for h in range(hours):
        for t in range(width // LANES):
            sl = slice(t * LANES, (t + 1) * LANES)
            c, d = (
                sum(t_ref[n, z, h, :ports].astype(F32) for z in range(t_ref.shape[1])) for n in (2 * t, 2 * t + 1)
            )
            k_ref[h, :, sl] = jnp.where(low, c, swap(d)).astype(BF16)
            v_ref[h, :, sl] = jnp.where(low, swap(c), d).astype(BF16)
            a, b = (t_ref[n, z_own, h, ports : ports + half].astype(F32) for n in (2 * t, 2 * t + 1))
            q_ref[h, :half, sl] = jnp.where(lh, a, swap(b)).astype(BF16)
            q_ref[h, half:, sl] = jnp.where(lh, swap(a), b).astype(BF16)


def call(kernel, outs, *args, scratch=(), name):
    return pl.pallas_call(
        kernel,
        out_shape=outs,
        scratch_shapes=scratch,
        compiler_params=pltpu.CompilerParams(vmem_limit_bytes=40 * 1024 * 1024),
        name=name,
    )(*args)


def shape(*dims):
    return jax.ShapeDtypeStruct(dims, BF16)


def exchange(a, axes):
    return lax.all_to_all(a, axes, 0, 0, tiled=True)


def per_device(query_rows, key_rows, value_rows, out_grad, out_weight, adjacency):
    parts = lax.axis_size("zh")
    heads, hours = lax.axis_size("x"), lax.axis_size("c")
    port_count = lax.axis_size(PORT_AXES)
    tm_count = lax.axis_size(TM_AXES)
    ports, _, width = query_rows.shape
    model = out_grad.shape[2]
    group = heads * hours
    total = port_count * ports
    q, k, v, g = (a.transpose(1, 0, 2) for a in (query_rows, key_rows, value_rows, out_grad))
    kv_send = call(pack_kv_kernel, shape(heads, hours, ports, LANES), k, v, name="pack_kv")
    kv0 = exchange(kv_send.reshape(group, ports, LANES), ("x", "c"))
    adj = jnp.pad(adjacency, ((0, 0), (HEAD_DIM, LANES - HEAD_DIM - adjacency.shape[1])))
    qg_send = call(pack_qg_kernel, shape(heads, hours, ports, LANES + model), q, g, adj, name="pack_qg")
    kv0, qg_send = lax.optimization_barrier((kv0, qg_send))
    kv_all = lax.all_gather(kv0, "zh")
    qg_got = exchange(qg_send.reshape(group, ports, LANES + model), ("x", "c"))
    w_n = lax.dynamic_slice_in_dim(out_weight, lax.axis_index("x") * HEAD_DIM, HEAD_DIM, 0)
    tiles = HEAD_DIM * model // (8 * LANES)
    chunk = ports + ports // 2 + 8
    vec, acc = pltpu.VMEM((total, LANES), BF16), pltpu.VMEM((HEAD_DIM, total), F32)
    back, dw = call(
        functools.partial(attend_kernel, 256),
        (shape(heads, parts, hours, chunk, LANES), shape(tiles, 8, LANES)),
        kv_all,
        qg_got,
        w_n,
        scratch=[vec, vec, acc, acc],
        name="attend",
    )
    dw = exchange(dw, TM_AXES)
    dw = jnp.sum(dw.astype(F32), axis=0).astype(BF16)
    back = back.reshape(port_count, chunk, LANES)
    back = back.at[:, chunk - 8 :, :].set(jnp.broadcast_to(dw, (port_count, 8, LANES)))
    back = exchange(back, PORT_AXES).reshape(heads, parts, hours, chunk, LANES)
    dw = back[:, :, :, chunk - 8 :, :].astype(F32)
    dw = (jnp.sum(dw, axis=(1, 2)) * (1.0 / (hours * tm_count))).astype(BF16)
    dw = exchange(jnp.broadcast_to(dw, (tm_count, *dw.shape)), TM_AXES)
    dw = dw.transpose(1, 0, 2, 3).reshape(heads, HEAD_DIM // 8, model // LANES, 8, LANES)
    dw = dw.transpose(0, 1, 3, 2, 4).reshape(width, model).astype(F32)
    vmem = pl.BlockSpec(memory_space=pltpu.VMEM)
    grads = pl.pallas_call(
        unpack_kernel,
        out_shape=(shape(hours, ports, width),) * 3,
        in_specs=[pl.BlockSpec(memory_space=pltpu.SMEM), vmem],
        out_specs=(vmem,) * 3,
        compiler_params=pltpu.CompilerParams(vmem_limit_bytes=40 * 1024 * 1024),
        name="unpack",
    )(lax.axis_index("zh").reshape(1), back)
    return *(a.transpose(1, 0, 2) for a in grads), dw


def solution(mesh):
    fine = Mesh(mesh.devices.reshape(4, 3, 2, 8, 4), PORT_AXES + TM_AXES)
    rows = P(PORT_AXES, TM_AXES, None)
    return jax.shard_map(
        per_device,
        mesh=fine,
        in_specs=(rows, rows, rows, rows, P(), P(PORT_AXES, None)),
        out_specs=(rows, rows, rows, P()),
        check_vma=False,
    )
```

```python
import jax
import jax.numpy as jnp
from jax import lax
from jax.experimental import pallas as pl
from jax.experimental.pallas import tpu as pltpu
from jax.sharding import Mesh, PartitionSpec as P

HEAD_DIM = 64
BLK = 32
LANES = 128
LOG2E = 1.4426950408889634
BIG = 1e30
F32, BF16 = jnp.float32, jnp.bfloat16

PORT_AXES = ("x", "zh", "c")
TM_AXES = ("y", "zl")
NT = (((1,), (1,)), ((), ()))
NN = (((1,), (0,)), ((), ()))
TN = (((0,), (0,)), ((), ()))


def dot(a, b, dims):
    return lax.dot_general(a, b, dims, preferred_element_type=F32)


def low_half(rows):
    return lax.broadcasted_iota(jnp.int32, (rows, LANES), 1) < HEAD_DIM


def swap(a):
    return jnp.concatenate([a[:, HEAD_DIM:], a[:, :HEAD_DIM]], axis=1)


def pack_kv_kernel(k_ref, v_ref, out_ref):
    hours, ports, width = k_ref.shape
    low = low_half(ports)
    for h in range(hours):
        for t in range(width // LANES):
            cols = slice(t * LANES, (t + 1) * LANES)
            k, v = k_ref[h, :, cols].astype(F32), v_ref[h, :, cols].astype(F32)
            even = jnp.where(low, k, swap(v)).astype(BF16)
            odd = jnp.where(low, swap(k), v).astype(BF16)
            for z in range(out_ref.shape[1]):
                out_ref[2 * t, z, h] = even
                out_ref[2 * t + 1, z, h] = odd


def pack_qg_kernel(q_ref, g_ref, adj_ref, out_ref):
    hours, ports, width = q_ref.shape
    low = low_half(ports)
    bias = (adj_ref[...].astype(F32) - 1.0) * BIG
    bias = jnp.concatenate(
        [jnp.broadcast_to(bias[b : b + 1, :], (BLK, LANES)) for b in range(ports // BLK)], axis=0
    )
    for h in range(hours):
        for t in range(width // LANES):
            q = q_ref[h, :, t * LANES : (t + 1) * LANES].astype(F32)
            at = 2 * t * LANES
            out_ref[h, :, at : at + LANES] = jnp.where(low, q, bias).astype(BF16)
            out_ref[h, :, at + LANES : at + 2 * LANES] = jnp.where(low, swap(q), bias).astype(BF16)
        out_ref[h, :, 2 * width :] = g_ref[h]


def route_kernel(at_ref, qg_ref, *out_refs):
    heads = len(out_refs)
    hour = at_ref[1]
    for s, out_ref in enumerate(out_refs):
        n = lax.rem(at_ref[0] + s, heads)
        for c in range(qg_ref.shape[0]):
            out_ref[c, :, :LANES] = qg_ref[c, hour, :, pl.ds(pl.multiple_of(n * LANES, LANES), LANES)]
            out_ref[c, :, LANES:] = qg_ref[c, hour, :, heads * LANES :]


def attend_kernel(kv_ref, p0_ref, p1_ref, p2_ref, p3_ref, w_ref, out_ref, dq_ref, dw_ref, kx, kv, dkt, dvt):
    sources, ports, _ = kv_ref.shape
    total = sources * ports
    parts = (p0_ref, p1_ref, p2_ref, p3_ref)
    own = len(parts) * 2 * ports
    rows = 4 * ports
    part = kv_ref[...].reshape(total, LANES)
    lane = lax.broadcasted_iota(jnp.int32, (total, LANES), 1)
    block = lax.shift_right_logical(lax.broadcasted_iota(jnp.int32, (total, LANES), 0), 5)
    hot = jnp.where(lane - HEAD_DIM == block, 1.0, 0.0)
    kv[...] = part
    kx[...] = jnp.where(lane < HEAD_DIM, part.astype(F32), hot).astype(BF16)
    w_n = jnp.concatenate([jnp.zeros_like(w_ref), w_ref[...]], axis=0)
    scale2 = 0.125 * LOG2E
    low = low_half(rows)
    per = rows // ports
    dw = None
    for b in range(own // rows):
        mine = jnp.concatenate([parts[2 * b][...], parts[2 * b + 1][...]], axis=0)
        qx = mine[:, :, :LANES].reshape(rows, LANES)
        g = mine[:, :, LANES:].reshape(rows, -1)
        d = dot(g, w_n, NT).astype(BF16)
        s = dot(qx, kx[...], NT)
        top = jnp.max(s, axis=1, keepdims=True)
        e = jnp.exp2((s - top) * scale2)
        p = e * (1.0 / jnp.sum(e, axis=1, keepdims=True))
        p_low = p.astype(BF16)
        att = dot(p_low, kv[...], NN).astype(BF16)
        part = dot(att, g, TN)
        dw = part if dw is None else dw + part
        d32 = d.astype(F32)
        term = jnp.sum(d32 * att.astype(F32), axis=1, keepdims=True)
        dp = dot(d, kv[...], NT)
        ds = (p * (dp - term)).astype(BF16)
        dq = dot(ds, kv[...], NN) * 0.125
        qdt = jnp.where(low, qx.astype(F32), d32).T.astype(BF16)
        dk_part = dot(qdt[:HEAD_DIM], ds, NN)
        dv_part = dot(qdt[HEAD_DIM:], p_low, NN)
        if b:
            dkt[...] += dk_part
            dvt[...] += dv_part
        else:
            dkt[...] = dk_part
            dvt[...] = dv_part
        half = ports // 2
        for i in range(per):
            a, c = dq[i * ports : i * ports + half], dq[i * ports + half : (i + 1) * ports]
            dq_ref[i % 2, (b * per + i) // 2] = jnp.where(low_half(half), a, swap(c)).astype(BF16)
    dw = dw[HEAD_DIM:].astype(BF16)
    wide = dw.shape[1] // LANES
    for r in range(HEAD_DIM // 8):
        for c in range(wide):
            dw_ref[r * wide + c] = dw[r * 8 : (r + 1) * 8, c * LANES : (c + 1) * LANES]
    both = jnp.concatenate([dkt[...] * 0.125, dvt[...]], axis=0).T.astype(BF16)
    for i in range(sources):
        out_ref[i, :ports, :] = both[i * ports : (i + 1) * ports]
        out_ref[i, ports:, :] = jnp.zeros((8, LANES), BF16)


def unpack_kernel(x_ref, t_ref, d0_ref, d1_ref, d2_ref, d3_ref, q_ref, k_ref, v_ref, dq):
    hours, ports, width = q_ref.shape
    low = low_half(ports)
    half = ports // 2
    lh = low_half(half)
    for s, ref in enumerate((d0_ref, d1_ref, d2_ref, d3_ref)):
        dq[lax.rem(x_ref[0] + s, 4)] = ref[...]
    for h in range(hours):
        for t in range(width // LANES):
            sl = slice(t * LANES, (t + 1) * LANES)
            c, d = (
                sum(t_ref[n, z, h, :ports].astype(F32) for z in range(t_ref.shape[1])) for n in (2 * t, 2 * t + 1)
            )
            k_ref[h, :, sl] = jnp.where(low, c, swap(d)).astype(BF16)
            v_ref[h, :, sl] = jnp.where(low, swap(c), d).astype(BF16)
            a, b = (dq[n, h].astype(F32) for n in (2 * t, 2 * t + 1))
            q_ref[h, :half, sl] = jnp.where(lh, a, swap(b)).astype(BF16)
            q_ref[h, half:, sl] = jnp.where(lh, swap(a), b).astype(BF16)


def call(kernel, outs, *args, scratch=(), scalars=0, name):
    smem, vmem = pl.BlockSpec(memory_space=pltpu.SMEM), pl.BlockSpec(memory_space=pltpu.VMEM)
    return pl.pallas_call(
        kernel,
        out_shape=outs,
        in_specs=[smem] * scalars + [vmem] * (len(args) - scalars),
        out_specs=jax.tree.map(lambda _: vmem, outs),
        scratch_shapes=scratch,
        compiler_params=pltpu.CompilerParams(vmem_limit_bytes=40 * 1024 * 1024),
        name=name,
    )(*args)


def shape(*dims):
    return jax.ShapeDtypeStruct(dims, BF16)


def exchange(a, axes):
    return lax.all_to_all(a, axes, 0, 0, tiled=True)


def along_x(a, by):
    heads = lax.axis_size("x")
    return lax.ppermute(a, "x", [(i, (i + by) % heads) for i in range(heads)])


def per_device(query_rows, key_rows, value_rows, out_grad, out_weight, adjacency):
    parts = lax.axis_size("zh")
    heads, hours = lax.axis_size("x"), lax.axis_size("c")
    port_count = lax.axis_size(PORT_AXES)
    tm_count = lax.axis_size(TM_AXES)
    ports, _, width = query_rows.shape
    model = out_grad.shape[2]
    total = port_count * ports
    x, core = lax.axis_index("x"), lax.axis_index("c")
    q, k, v, g = (a.transpose(1, 0, 2) for a in (query_rows, key_rows, value_rows, out_grad))
    kv_send = call(pack_kv_kernel, shape(heads, parts, hours, ports, LANES), k, v, name="pack_kv")
    kv_got = exchange(kv_send.reshape(port_count, ports, LANES), PORT_AXES)
    adj = jnp.pad(adjacency, ((0, 0), (HEAD_DIM, LANES - HEAD_DIM - adjacency.shape[1])))
    qg = call(pack_qg_kernel, shape(hours, ports, heads * LANES + model), q, g, adj, name="pack_qg")
    qg = lax.all_gather(qg, "c")
    routed = call(
        route_kernel,
        (shape(hours, ports, LANES + model),) * heads,
        jnp.stack([x, core]),
        qg,
        scalars=1,
        name="route",
    )
    routed = [a if s == 0 else along_x(a, s) for s, a in enumerate(routed)]
    w_n = lax.dynamic_slice_in_dim(out_weight, x * HEAD_DIM, HEAD_DIM, 0)
    tiles = HEAD_DIM * model // (8 * LANES)
    chunk = ports + 8
    vec, acc = pltpu.VMEM((total, LANES), BF16), pltpu.VMEM((HEAD_DIM, total), F32)
    back, dq, dw = call(
        attend_kernel,
        (shape(port_count, chunk, LANES), shape(hours, heads, ports // 2, LANES), shape(tiles, 8, LANES)),
        kv_got,
        *routed,
        w_n,
        scratch=[vec, vec, acc, acc],
        name="attend",
    )
    dw = exchange(dw, TM_AXES)
    dw = jnp.sum(dw.astype(F32), axis=0).astype(BF16)
    dq = lax.dynamic_index_in_dim(lax.all_gather(dq, "c"), core, 1, keepdims=False)
    dq = [dq[:, s] if s == 0 else along_x(dq[:, s], heads - s) for s in range(heads)]
    back = back.at[:, chunk - 8 :, :].set(jnp.broadcast_to(dw, (port_count, 8, LANES)))
    back, dq = lax.optimization_barrier((exchange(back, PORT_AXES), dq))
    back = back.reshape(heads, parts, hours, chunk, LANES)
    dw = back[:, :, :, chunk - 8 :, :].astype(F32)
    dw = (jnp.sum(dw, axis=(1, 2)) * (1.0 / (hours * tm_count))).astype(BF16)
    dw = exchange(jnp.broadcast_to(dw, (tm_count, *dw.shape)), TM_AXES)
    dw = dw.transpose(1, 0, 2, 3).reshape(heads, HEAD_DIM // 8, model // LANES, 8, LANES)
    dw = dw.transpose(0, 1, 3, 2, 4).reshape(width, model).astype(F32)
    grads = call(
        unpack_kernel,
        (shape(hours, ports, width),) * 3,
        x.reshape(1),
        back,
        *dq,
        scratch=[pltpu.VMEM((heads, hours, ports // 2, LANES), BF16)],
        scalars=1,
        name="unpack",
    )
    return *(a.transpose(1, 0, 2) for a in grads), dw


def solution(mesh):
    fine = Mesh(mesh.devices.reshape(4, 3, 2, 8, 4), PORT_AXES + TM_AXES)
    rows = P(PORT_AXES, TM_AXES, None)
    return jax.shard_map(
        per_device,
        mesh=fine,
        in_specs=(rows, rows, rows, rows, P(), P(PORT_AXES, None)),
        out_specs=(rows, rows, rows, P()),
        check_vma=False,
    )
```

```python
import jax
import jax.numpy as jnp
from jax import lax
from jax.experimental import pallas as pl
from jax.experimental.pallas import tpu as pltpu
from jax.sharding import Mesh, PartitionSpec as P

HEAD_DIM = 64
BLK = 32
LANES = 128
LOG2E = 1.4426950408889634
BIG = 1e30
F32, BF16 = jnp.float32, jnp.bfloat16

PORT_AXES = ("x", "zh", "c")
TM_AXES = ("y", "zl")
NT = (((1,), (1,)), ((), ()))
NN = (((1,), (0,)), ((), ()))
TN = (((0,), (0,)), ((), ()))


def dot(a, b, dims):
    return lax.dot_general(a, b, dims, preferred_element_type=F32)


def low_half(rows):
    return lax.broadcasted_iota(jnp.int32, (rows, LANES), 1) < HEAD_DIM


def swap(a):
    return jnp.concatenate([a[:, HEAD_DIM:], a[:, :HEAD_DIM]], axis=1)


def pack_kv_kernel(k_ref, v_ref, out_ref):
    hours, ports, width = k_ref.shape
    low = low_half(ports)
    for h in range(hours):
        for t in range(width // LANES):
            cols = slice(t * LANES, (t + 1) * LANES)
            k, v = k_ref[h, :, cols].astype(F32), v_ref[h, :, cols].astype(F32)
            even = jnp.where(low, k, swap(v)).astype(BF16)
            odd = jnp.where(low, swap(k), v).astype(BF16)
            for z in range(out_ref.shape[1]):
                out_ref[2 * t, z, h] = even
                out_ref[2 * t + 1, z, h] = odd


def pack_qg_kernel(q_ref, g_ref, adj_ref, out_ref):
    hours, ports, width = q_ref.shape
    low = low_half(ports)
    bias = (adj_ref[...].astype(F32) - 1.0) * BIG
    bias = jnp.concatenate(
        [jnp.broadcast_to(bias[b : b + 1, :], (BLK, LANES)) for b in range(ports // BLK)], axis=0
    )
    for h in range(hours):
        for t in range(width // LANES):
            q = q_ref[h, :, t * LANES : (t + 1) * LANES].astype(F32)
            at = 2 * t * LANES
            out_ref[h, :, at : at + LANES] = jnp.where(low, q, bias).astype(BF16)
            out_ref[h, :, at + LANES : at + 2 * LANES] = jnp.where(low, swap(q), bias).astype(BF16)
        out_ref[h, :, 2 * width :] = g_ref[h]


def route_kernel(at_ref, qg_ref, *out_refs):
    heads = len(out_refs)
    hour = at_ref[1]
    for s, out_ref in enumerate(out_refs):
        n = lax.rem(at_ref[0] + s, heads)
        for c in range(qg_ref.shape[0]):
            out_ref[c, :, :LANES] = qg_ref[c, hour, :, pl.ds(pl.multiple_of(n * LANES, LANES), LANES)]
            out_ref[c, :, LANES:] = qg_ref[c, hour, :, heads * LANES :]


def attend_kernel(kv_ref, p0_ref, p1_ref, p2_ref, p3_ref, w_ref, out_ref, dq_ref, dw_ref, kx, kv, dkt, dvt):
    sources, ports, _ = kv_ref.shape
    total = sources * ports
    parts = (p0_ref, p1_ref, p2_ref, p3_ref)
    own = len(parts) * 2 * ports
    rows = 4 * ports
    part = kv_ref[...].reshape(total, LANES)
    lane = lax.broadcasted_iota(jnp.int32, (total, LANES), 1)
    block = lax.shift_right_logical(lax.broadcasted_iota(jnp.int32, (total, LANES), 0), 5)
    hot = jnp.where(lane - HEAD_DIM == block, 1.0, 0.0)
    kv[...] = part
    kx[...] = jnp.where(lane < HEAD_DIM, part.astype(F32), hot).astype(BF16)
    w_n = jnp.concatenate([jnp.zeros_like(w_ref), w_ref[...]], axis=0)
    scale2 = 0.125 * LOG2E
    low = low_half(rows)
    per = rows // ports
    dw = None
    for b in range(own // rows):
        mine = jnp.concatenate([parts[2 * b][...], parts[2 * b + 1][...]], axis=0)
        qx = mine[:, :, :LANES].reshape(rows, LANES)
        g = mine[:, :, LANES:].reshape(rows, -1)
        d = dot(g, w_n, NT).astype(BF16)
        s = dot(qx, kx[...], NT)
        top = jnp.max(s, axis=1, keepdims=True)
        e = jnp.exp2((s - top) * scale2)
        p = e * (1.0 / jnp.sum(e, axis=1, keepdims=True))
        p_low = p.astype(BF16)
        att = dot(p_low, kv[...], NN).astype(BF16)
        part = dot(att, g, TN)
        dw = part if dw is None else dw + part
        d32 = d.astype(F32)
        term = jnp.sum(d32 * att.astype(F32), axis=1, keepdims=True)
        dp = dot(d, kv[...], NT)
        ds = (p * (dp - term)).astype(BF16)
        dq = dot(ds, kv[...], NN) * 0.125
        qdt = jnp.where(low, qx.astype(F32), d32).T.astype(BF16)
        dk_part = dot(qdt[:HEAD_DIM], ds, NN)
        dv_part = dot(qdt[HEAD_DIM:], p_low, NN)
        if b:
            dkt[...] += dk_part
            dvt[...] += dv_part
        else:
            dkt[...] = dk_part
            dvt[...] = dv_part
        half = ports // 2
        for i in range(per):
            a, c = dq[i * ports : i * ports + half], dq[i * ports + half : (i + 1) * ports]
            dq_ref[i % 2, (b * per + i) // 2] = jnp.where(low_half(half), a, swap(c)).astype(BF16)
    dw = dw[HEAD_DIM:].astype(BF16)
    wide = dw.shape[1] // LANES
    for r in range(HEAD_DIM // 8):
        for c in range(wide):
            dw_ref[r * wide + c] = dw[r * 8 : (r + 1) * 8, c * LANES : (c + 1) * LANES]
    both = jnp.concatenate([dkt[...] * 0.125, dvt[...]], axis=0).T.astype(BF16)
    thirds, pair = out_ref.shape[0], 2 * ports
    for i in range(sources // 2):
        at = (i // thirds) * pair
        out_ref[i % thirds, at : at + pair, :] = both[i * pair : (i + 1) * pair]


def merge_kernel(x_ref, kv_ref, dq_ref, out_ref):
    heads, cores, ports, _ = kv_ref.shape
    for s in range(heads):
        to = lax.rem(x_ref[0] + heads - s, heads)
        for c in range(cores):
            out_ref[s, c, :ports, :] = kv_ref[to, c]
            out_ref[s, c, ports:, :] = dq_ref[c, s]


def unpack_kernel(x_ref, d0_ref, d1_ref, d2_ref, d3_ref, q_ref, k_ref, v_ref, all_ref):
    hours, ports, width = q_ref.shape
    low = low_half(ports)
    half = ports // 2
    lh = low_half(half)
    for s, ref in enumerate((d0_ref, d1_ref, d2_ref, d3_ref)):
        all_ref[lax.rem(x_ref[0] + s, 4)] = ref[...]
    for h in range(hours):
        for t in range(width // LANES):
            sl = slice(t * LANES, (t + 1) * LANES)
            c, d = (all_ref[n, h, :ports].astype(F32) for n in (2 * t, 2 * t + 1))
            k_ref[h, :, sl] = jnp.where(low, c, swap(d)).astype(BF16)
            v_ref[h, :, sl] = jnp.where(low, swap(c), d).astype(BF16)
            a, b = (all_ref[n, h, ports:].astype(F32) for n in (2 * t, 2 * t + 1))
            q_ref[h, :half, sl] = jnp.where(lh, a, swap(b)).astype(BF16)
            q_ref[h, half:, sl] = jnp.where(lh, swap(a), b).astype(BF16)


def call(kernel, outs, *args, scratch=(), scalars=0, name):
    smem, vmem = pl.BlockSpec(memory_space=pltpu.SMEM), pl.BlockSpec(memory_space=pltpu.VMEM)
    return pl.pallas_call(
        kernel,
        out_shape=outs,
        in_specs=[smem] * scalars + [vmem] * (len(args) - scalars),
        out_specs=jax.tree.map(lambda _: vmem, outs),
        scratch_shapes=scratch,
        compiler_params=pltpu.CompilerParams(vmem_limit_bytes=40 * 1024 * 1024),
        name=name,
    )(*args)


def shape(*dims):
    return jax.ShapeDtypeStruct(dims, BF16)


def exchange(a, axes):
    return lax.all_to_all(a, axes, 0, 0, tiled=True)


def along_x(a, by):
    heads = lax.axis_size("x")
    return lax.ppermute(a, "x", [(i, (i + by) % heads) for i in range(heads)])


def per_device(query_rows, key_rows, value_rows, out_grad, out_weight, adjacency):
    parts = lax.axis_size("zh")
    heads, hours = lax.axis_size("x"), lax.axis_size("c")
    port_count = lax.axis_size(PORT_AXES)
    tm_count = lax.axis_size(TM_AXES)
    ports, _, width = query_rows.shape
    model = out_grad.shape[2]
    total = port_count * ports
    x, core = lax.axis_index("x"), lax.axis_index("c")
    q, k, v, g = (a.transpose(1, 0, 2) for a in (query_rows, key_rows, value_rows, out_grad))
    kv_send = call(pack_kv_kernel, shape(heads, parts, hours, ports, LANES), k, v, name="pack_kv")
    kv_got = exchange(kv_send.reshape(port_count, ports, LANES), PORT_AXES)
    adj = jnp.pad(adjacency, ((0, 0), (HEAD_DIM, LANES - HEAD_DIM - adjacency.shape[1])))
    qg = call(pack_qg_kernel, shape(hours, ports, heads * LANES + model), q, g, adj, name="pack_qg")
    qg = lax.all_gather(qg, "c")
    routed = call(
        route_kernel,
        (shape(hours, ports, LANES + model),) * heads,
        jnp.stack([x, core]),
        qg,
        scalars=1,
        name="route",
    )
    routed = [a if s == 0 else along_x(a, s) for s, a in enumerate(routed)]
    w_n = lax.dynamic_slice_in_dim(out_weight, x * HEAD_DIM, HEAD_DIM, 0)
    tiles = HEAD_DIM * model // (8 * LANES)
    rows = ports + ports // 2
    vec, acc = pltpu.VMEM((total, LANES), BF16), pltpu.VMEM((HEAD_DIM, total), F32)
    dkv, dq, dw = call(
        attend_kernel,
        (shape(parts, total // parts, LANES), shape(hours, heads, ports // 2, LANES), shape(tiles, 8, LANES)),
        kv_got,
        *routed,
        w_n,
        scratch=[vec, vec, acc, acc],
        name="attend",
    )
    dw = exchange(dw, TM_AXES)
    dw = jnp.sum(dw.astype(F32), axis=0).astype(BF16)
    dkv = lax.psum_scatter(dkv.reshape(total, LANES), "zh", scatter_dimension=0, tiled=True)
    dw = exchange(jnp.broadcast_to(dw, (port_count, 8, LANES)), PORT_AXES)
    dw, dq = lax.optimization_barrier((dw, dq))
    dw = dw.reshape(heads, parts, hours, 8, LANES).astype(F32)
    dw = (jnp.sum(dw, axis=(1, 2)) * (1.0 / (hours * tm_count))).astype(BF16)
    dw = exchange(jnp.broadcast_to(dw, (tm_count, *dw.shape)), TM_AXES)
    dw = dw.transpose(1, 0, 2, 3).reshape(heads, HEAD_DIM // 8, model // LANES, 8, LANES)
    dw = dw.transpose(0, 1, 3, 2, 4).reshape(width, model).astype(F32)
    both = call(
        merge_kernel,
        shape(heads, hours, rows, LANES),
        x.reshape(1),
        dkv.reshape(heads, hours, ports, LANES),
        dq,
        scalars=1,
        name="merge",
    )
    both = lax.dynamic_index_in_dim(lax.all_gather(both, "c"), core, 2, keepdims=False)
    both = [both[:, s] if s == 0 else along_x(both[:, s], heads - s) for s in range(heads)]
    grads = call(
        unpack_kernel,
        (shape(hours, ports, width),) * 3,
        x.reshape(1),
        *both,
        scratch=[pltpu.VMEM((heads, hours, rows, LANES), BF16)],
        scalars=1,
        name="unpack",
    )
    return *(a.transpose(1, 0, 2) for a in grads), dw


def solution(mesh):
    fine = Mesh(mesh.devices.reshape(4, 3, 2, 8, 4), PORT_AXES + TM_AXES)
    rows = P(PORT_AXES, TM_AXES, None)
    return jax.shard_map(
        per_device,
        mesh=fine,
        in_specs=(rows, rows, rows, rows, P(), P(PORT_AXES, None)),
        out_specs=(rows, rows, rows, P()),
        check_vma=False,
    )
```

```python
import functools

import jax
import jax.numpy as jnp
from jax import lax
from jax.experimental import pallas as pl
from jax.experimental.pallas import tpu as pltpu
from jax.sharding import Mesh, PartitionSpec as P

HEAD_DIM = 64
BLK = 32
LANES = 128
LOG2E = 1.4426950408889634
BIG = 1e30
F32, BF16 = jnp.float32, jnp.bfloat16

PORT_AXES = ("x", "zh", "c")
TM_AXES = ("y", "zl")
NT = (((1,), (1,)), ((), ()))
NN = (((1,), (0,)), ((), ()))
TN = (((0,), (0,)), ((), ()))


def dot(a, b, dims):
    return lax.dot_general(a, b, dims, preferred_element_type=F32)


def low_half(rows):
    return lax.broadcasted_iota(jnp.int32, (rows, LANES), 1) < HEAD_DIM


def swap(a):
    return jnp.concatenate([a[:, HEAD_DIM:], a[:, :HEAD_DIM]], axis=1)


def pack_kv_kernel(k_ref, v_ref, out_ref):
    ports, hours, width = k_ref.shape
    low = low_half(ports)
    k_all, v_all = k_ref[...].astype(F32), v_ref[...].astype(F32)
    for h in range(hours):
        for t in range(width // LANES):
            cols = slice(t * LANES, (t + 1) * LANES)
            k, v = k_all[:, h, cols], v_all[:, h, cols]
            even = jnp.where(low, k, swap(v)).astype(BF16)
            odd = jnp.where(low, swap(k), v).astype(BF16)
            for z in range(out_ref.shape[1]):
                out_ref[2 * t, z, h] = even
                out_ref[2 * t + 1, z, h] = odd


def pack_qg_kernel(q_ref, g_ref, adj_ref, out_ref):
    hours, ports, width = q_ref.shape
    low = low_half(ports)
    bias = (adj_ref[...].astype(F32) - 1.0) * BIG
    bias = jnp.concatenate(
        [jnp.broadcast_to(bias[b : b + 1, :], (BLK, LANES)) for b in range(ports // BLK)], axis=0
    )
    for h in range(hours):
        for t in range(width // LANES):
            q = q_ref[h, :, t * LANES : (t + 1) * LANES].astype(F32)
            at = 2 * t * LANES
            out_ref[h, :, at : at + LANES] = jnp.where(low, q, bias).astype(BF16)
            out_ref[h, :, at + LANES : at + 2 * LANES] = jnp.where(low, swap(q), bias).astype(BF16)
        out_ref[h, :, 2 * width :] = g_ref[h]


def route_kernel(at_ref, qg_ref, *out_refs):
    heads = len(out_refs)
    hour = at_ref[1]
    for s, out_ref in enumerate(out_refs):
        n = lax.bitwise_xor(at_ref[0], s)
        for c in range(qg_ref.shape[0]):
            out_ref[c, :, :LANES] = qg_ref[c, hour, :, pl.ds(pl.multiple_of(n * LANES, LANES), LANES)]
            out_ref[c, :, LANES:] = qg_ref[c, hour, :, heads * LANES :]


def attend_kernel(kv_ref, p0_ref, p1_ref, p2_ref, p3_ref, w_ref, out_ref, dq_ref, dw_ref, kx, kv, dkt, dvt):
    sources, ports, _ = kv_ref.shape
    total = sources * ports
    parts = (p0_ref, p1_ref, p2_ref, p3_ref)
    own = len(parts) * 2 * ports
    rows = 4 * ports
    part = kv_ref[...].reshape(total, LANES)
    lane = lax.broadcasted_iota(jnp.int32, (total, LANES), 1)
    block = lax.shift_right_logical(lax.broadcasted_iota(jnp.int32, (total, LANES), 0), 5)
    hot = jnp.where(lane - HEAD_DIM == block, 1.0, 0.0)
    kv[...] = part
    kx[...] = jnp.where(lane < HEAD_DIM, part.astype(F32), hot).astype(BF16)
    w_n = jnp.concatenate([jnp.zeros_like(w_ref), w_ref[...]], axis=0)
    scale2 = 0.125 * LOG2E
    low = low_half(rows)
    per = rows // ports
    dw = None
    for b in range(own // rows):
        mine = jnp.concatenate([parts[2 * b][...], parts[2 * b + 1][...]], axis=0)
        qx = mine[:, :, :LANES].reshape(rows, LANES)
        g = mine[:, :, LANES:].reshape(rows, -1)
        d = dot(g, w_n, NT).astype(BF16)
        s = dot(qx, kx[...], NT)
        top = jnp.max(s, axis=1, keepdims=True)
        e = jnp.exp2((s - top) * scale2)
        p = e * (1.0 / jnp.sum(e, axis=1, keepdims=True))
        p_low = p.astype(BF16)
        att = dot(p_low, kv[...], NN).astype(BF16)
        part = dot(att, g, TN)
        dw = part if dw is None else dw + part
        d32 = d.astype(F32)
        term = jnp.sum(d32 * att.astype(F32), axis=1, keepdims=True)
        dp = dot(d, kv[...], NT)
        ds = (p * (dp - term)).astype(BF16)
        dq = dot(ds, kv[...], NN) * 0.125
        qdt = jnp.where(low, qx.astype(F32), d32).T.astype(BF16)
        dk_part = dot(qdt[:HEAD_DIM], ds, NN)
        dv_part = dot(qdt[HEAD_DIM:], p_low, NN)
        if b:
            dkt[...] += dk_part
            dvt[...] += dv_part
        else:
            dkt[...] = dk_part
            dvt[...] = dv_part
        half = ports // 2
        for i in range(per):
            a, c = dq[i * ports : i * ports + half], dq[i * ports + half : (i + 1) * ports]
            dq_ref[i % 2, (b * per + i) // 2] = jnp.where(low_half(half), a, swap(c)).astype(BF16)
    dw = dw[HEAD_DIM:].astype(BF16)
    wide = dw.shape[1] // LANES
    for r in range(HEAD_DIM // 8):
        for c in range(wide):
            dw_ref[r * wide + c] = dw[r * 8 : (r + 1) * 8, c * LANES : (c + 1) * LANES]
    both = jnp.concatenate([dkt[...] * 0.125, dvt[...]], axis=0).T.astype(BF16)
    for i in range(sources):
        out_ref[i, :ports, :] = both[i * ports : (i + 1) * ports]
        out_ref[i, ports:, :] = jnp.zeros((8, LANES), BF16)


def unpack_kernel(x_ref, t_ref, d0_ref, d1_ref, d2_ref, d3_ref, q_ref, k_ref, v_ref, dq):
    hours, ports, width = q_ref.shape
    low = low_half(ports)
    half = ports // 2
    lh = low_half(half)
    for s, ref in enumerate((d0_ref, d1_ref, d2_ref, d3_ref)):
        dq[lax.bitwise_xor(x_ref[0], s)] = ref[...]
    for h in range(hours):
        for t in range(width // LANES):
            sl = slice(t * LANES, (t + 1) * LANES)
            c, d = (
                sum(t_ref[n, z, h, :ports].astype(F32) for z in range(t_ref.shape[1])) for n in (2 * t, 2 * t + 1)
            )
            k_ref[h, :, sl] = jnp.where(low, c, swap(d)).astype(BF16)
            v_ref[h, :, sl] = jnp.where(low, swap(c), d).astype(BF16)
            a, b = (dq[n, h].astype(F32) for n in (2 * t, 2 * t + 1))
            q_ref[h, :half, sl] = jnp.where(lh, a, swap(b)).astype(BF16)
            q_ref[h, half:, sl] = jnp.where(lh, swap(a), b).astype(BF16)


def spread_kernel(scale, t_ref, out_ref):
    heads, parts, hours, rows, _ = t_ref.shape
    for n in range(heads):
        tile = sum(t_ref[n, z, h, rows - 8 :].astype(F32) for z in range(parts) for h in range(hours))
        tile = (tile * scale).astype(BF16)
        for t in range(out_ref.shape[0]):
            out_ref[t, n] = tile


def lay_kernel(t_ref, out_ref):
    tiles, heads, _, _ = t_ref.shape
    wide = out_ref.shape[1] // LANES
    deep = tiles // wide * 8
    for n in range(heads):
        for t in range(tiles):
            r, c = n * deep + t // wide * 8, t % wide * LANES
            out_ref[r : r + 8, c : c + LANES] = t_ref[t, n].astype(F32)


def call(kernel, outs, *args, scratch=(), scalars=0, name):
    smem, vmem = pl.BlockSpec(memory_space=pltpu.SMEM), pl.BlockSpec(memory_space=pltpu.VMEM)
    return pl.pallas_call(
        kernel,
        out_shape=outs,
        in_specs=[smem] * scalars + [vmem] * (len(args) - scalars),
        out_specs=jax.tree.map(lambda _: vmem, outs),
        scratch_shapes=scratch,
        compiler_params=pltpu.CompilerParams(vmem_limit_bytes=40 * 1024 * 1024),
        name=name,
    )(*args)


def shape(*dims):
    return jax.ShapeDtypeStruct(dims, BF16)


def exchange(a, axes):
    return lax.all_to_all(a, axes, 0, 0, tiled=True)


def along_x(a, by):
    return lax.ppermute(a, "x", [(i, i ^ by) for i in range(lax.axis_size("x"))])


def per_device(query_rows, key_rows, value_rows, out_grad, out_weight, adjacency):
    parts = lax.axis_size("zh")
    heads, hours = lax.axis_size("x"), lax.axis_size("c")
    port_count = lax.axis_size(PORT_AXES)
    tm_count = lax.axis_size(TM_AXES)
    ports, _, width = query_rows.shape
    model = out_grad.shape[2]
    total = port_count * ports
    x, core = lax.axis_index("x"), lax.axis_index("c")
    q, g = (a.transpose(1, 0, 2) for a in (query_rows, out_grad))
    kv_send = call(pack_kv_kernel, shape(heads, parts, hours, ports, LANES), key_rows, value_rows, name="pack_kv")
    kv_got = exchange(kv_send.reshape(port_count, ports, LANES), PORT_AXES)
    adj = jnp.pad(adjacency, ((0, 0), (HEAD_DIM, LANES - HEAD_DIM - adjacency.shape[1])))
    qg = call(pack_qg_kernel, shape(hours, ports, heads * LANES + model), q, g, adj, name="pack_qg")
    qg = lax.all_gather(qg, "c")
    routed = call(
        route_kernel,
        (shape(hours, ports, LANES + model),) * heads,
        jnp.stack([x, core]),
        qg,
        scalars=1,
        name="route",
    )
    routed = [a if s == 0 else along_x(a, s) for s, a in enumerate(routed)]
    w_n = lax.dynamic_slice_in_dim(out_weight, x * HEAD_DIM, HEAD_DIM, 0)
    tiles = HEAD_DIM * model // (8 * LANES)
    chunk = ports + 8
    vec, acc = pltpu.VMEM((total, LANES), BF16), pltpu.VMEM((HEAD_DIM, total), F32)
    back, dq, dw = call(
        attend_kernel,
        (shape(port_count, chunk, LANES), shape(hours, heads, ports // 2, LANES), shape(tiles, 8, LANES)),
        kv_got,
        *routed,
        w_n,
        scratch=[vec, vec, acc, acc],
        name="attend",
    )
    dw = exchange(dw, TM_AXES)
    dw = jnp.sum(dw.astype(F32), axis=0).astype(BF16)
    dq = lax.dynamic_index_in_dim(lax.all_gather(dq, "c"), core, 1, keepdims=False)
    dq = [dq[:, s] if s == 0 else along_x(dq[:, s], s) for s in range(heads)]
    back = back.at[:, chunk - 8 :, :].set(jnp.broadcast_to(dw, (port_count, 8, LANES)))
    back, dq = lax.optimization_barrier((exchange(back, PORT_AXES), dq))
    back = back.reshape(heads, parts, hours, chunk, LANES)
    dw = call(
        functools.partial(spread_kernel, 1.0 / (hours * tm_count)),
        shape(tm_count, heads, 8, LANES),
        back,
        name="spread",
    )
    dw = exchange(dw, TM_AXES)
    dw = call(lay_kernel, jax.ShapeDtypeStruct((width, model), F32), dw, name="lay")
    grads = call(
        unpack_kernel,
        (shape(hours, ports, width),) * 3,
        x.reshape(1),
        back,
        *dq,
        scratch=[pltpu.VMEM((heads, hours, ports // 2, LANES), BF16)],
        scalars=1,
        name="unpack",
    )
    return *(a.transpose(1, 0, 2) for a in grads), dw


def solution(mesh):
    fine = Mesh(mesh.devices.reshape(4, 3, 2, 8, 4), PORT_AXES + TM_AXES)
    rows = P(PORT_AXES, TM_AXES, None)
    return jax.shard_map(
        per_device,
        mesh=fine,
        in_specs=(rows, rows, rows, rows, P(), P(PORT_AXES, None)),
        out_specs=(rows, rows, rows, P()),
        check_vma=False,
    )
```

```python
import jax
import jax.numpy as jnp
from jax import lax
from jax.experimental import pallas as pl
from jax.experimental.pallas import tpu as pltpu
from jax.sharding import Mesh, PartitionSpec as P

HEAD_DIM = 64
BLK = 32
LANES = 128
LOG2E = 1.4426950408889634
BIG = 1e30
F32, BF16 = jnp.float32, jnp.bfloat16

PORT_AXES = ("x", "zh", "c")
TM_AXES = ("y", "zl")
NT = (((1,), (1,)), ((), ()))
NN = (((1,), (0,)), ((), ()))
TN = (((0,), (0,)), ((), ()))


def dot(a, b, dims):
    return lax.dot_general(a, b, dims, preferred_element_type=F32)


def low_half(rows):
    return lax.broadcasted_iota(jnp.int32, (rows, LANES), 1) < HEAD_DIM


def swap(a):
    return jnp.concatenate([a[:, HEAD_DIM:], a[:, :HEAD_DIM]], axis=1)


def pack_kv_kernel(k_ref, v_ref, out_ref):
    hours, ports, width = k_ref.shape
    low = low_half(ports)
    for h in range(hours):
        for t in range(width // LANES):
            cols = slice(t * LANES, (t + 1) * LANES)
            k, v = k_ref[h, :, cols].astype(F32), v_ref[h, :, cols].astype(F32)
            even = jnp.where(low, k, swap(v)).astype(BF16)
            odd = jnp.where(low, swap(k), v).astype(BF16)
            for z in range(out_ref.shape[1]):
                out_ref[2 * t, z, h] = even
                out_ref[2 * t + 1, z, h] = odd


def pack_qg_kernel(q_ref, g_ref, adj_ref, out_ref):
    hours, ports, width = q_ref.shape
    low = low_half(ports)
    bias = (adj_ref[...].astype(F32) - 1.0) * BIG
    bias = jnp.concatenate(
        [jnp.broadcast_to(bias[b : b + 1, :], (BLK, LANES)) for b in range(ports // BLK)], axis=0
    )
    for h in range(hours):
        for t in range(width // LANES):
            q = q_ref[h, :, t * LANES : (t + 1) * LANES].astype(F32)
            at = 2 * t * LANES
            out_ref[h, :, at : at + LANES] = jnp.where(low, q, bias).astype(BF16)
            out_ref[h, :, at + LANES : at + 2 * LANES] = jnp.where(low, swap(q), bias).astype(BF16)
        out_ref[h, :, 2 * width :] = g_ref[h]


def route_kernel(at_ref, qg_ref, *out_refs):
    heads = len(out_refs)
    hour = at_ref[1]
    for s, out_ref in enumerate(out_refs):
        n = lax.rem(at_ref[0] + s, heads)
        for c in range(qg_ref.shape[0]):
            out_ref[c, :, :LANES] = qg_ref[c, hour, :, pl.ds(pl.multiple_of(n * LANES, LANES), LANES)]
            out_ref[c, :, LANES:] = qg_ref[c, hour, :, heads * LANES :]


def attend_kernel(kv_ref, p0_ref, p2_ref, p1_ref, p3_ref, w_ref, out_ref, dq_ref, dw_ref, kx, kv, dkt, dvt):
    sources, ports, _ = kv_ref.shape
    total = sources * ports
    parts = (p0_ref, p1_ref, p2_ref, p3_ref)
    own = len(parts) * 2 * ports
    rows = 4 * ports
    part = kv_ref[...].reshape(total, LANES)
    lane = lax.broadcasted_iota(jnp.int32, (total, LANES), 1)
    block = lax.shift_right_logical(lax.broadcasted_iota(jnp.int32, (total, LANES), 0), 5)
    hot = jnp.where(lane - HEAD_DIM == block, 1.0, 0.0)
    kv[...] = part
    kx[...] = jnp.where(lane < HEAD_DIM, part.astype(F32), hot).astype(BF16)
    w_n = jnp.concatenate([jnp.zeros_like(w_ref), w_ref[...]], axis=0)
    scale2 = 0.125 * LOG2E
    low = low_half(rows)
    per = rows // ports
    dw = None
    for b in range(own // rows):
        mine = jnp.concatenate([parts[2 * b][...], parts[2 * b + 1][...]], axis=0)
        qx = mine[:, :, :LANES].reshape(rows, LANES)
        g = mine[:, :, LANES:].reshape(rows, -1)
        d = dot(g, w_n, NT).astype(BF16)
        s = dot(qx, kx[...], NT)
        top = jnp.max(s, axis=1, keepdims=True)
        e = jnp.exp2((s - top) * scale2)
        p = e * (1.0 / jnp.sum(e, axis=1, keepdims=True))
        p_low = p.astype(BF16)
        att = dot(p_low, kv[...], NN).astype(BF16)
        part = dot(att, g, TN)
        dw = part if dw is None else dw + part
        d32 = d.astype(F32)
        term = jnp.sum(d32 * att.astype(F32), axis=1, keepdims=True)
        dp = dot(d, kv[...], NT)
        ds = (p * (dp - term)).astype(BF16)
        dq = dot(ds, kv[...], NN) * 0.125
        qdt = jnp.where(low, qx.astype(F32), d32).T.astype(BF16)
        dk_part = dot(qdt[:HEAD_DIM], ds, NN)
        dv_part = dot(qdt[HEAD_DIM:], p_low, NN)
        if b:
            dkt[...] += dk_part
            dvt[...] += dv_part
        else:
            dkt[...] = dk_part
            dvt[...] = dv_part
        half = ports // 2
        for i in range(per):
            a, c = dq[i * ports : i * ports + half], dq[i * ports + half : (i + 1) * ports]
            dq_ref[i % 2, (b * per + i) // 2] = jnp.where(low_half(half), a, swap(c)).astype(BF16)
    dw = dw[HEAD_DIM:].astype(BF16)
    wide = dw.shape[1] // LANES
    for r in range(HEAD_DIM // 8):
        for c in range(wide):
            dw_ref[r * wide + c] = dw[r * 8 : (r + 1) * 8, c * LANES : (c + 1) * LANES]
    both = jnp.concatenate([dkt[...] * 0.125, dvt[...]], axis=0).T.astype(BF16)
    for i in range(sources):
        out_ref[i, :ports, :] = both[i * ports : (i + 1) * ports]
        out_ref[i, ports:, :] = jnp.zeros((8, LANES), BF16)


def unpack_kernel(x_ref, t_ref, d0_ref, d1_ref, d2_ref, d3_ref, q_ref, k_ref, v_ref, dq):
    hours, ports, width = q_ref.shape
    low = low_half(ports)
    half = ports // 2
    lh = low_half(half)
    for s, ref in enumerate((d0_ref, d1_ref, d2_ref, d3_ref)):
        dq[lax.rem(x_ref[0] + s, 4)] = ref[...]
    for h in range(hours):
        for t in range(width // LANES):
            sl = slice(t * LANES, (t + 1) * LANES)
            c, d = (
                sum(t_ref[n, z, h, :ports].astype(F32) for z in range(t_ref.shape[1])) for n in (2 * t, 2 * t + 1)
            )
            k_ref[h, :, sl] = jnp.where(low, c, swap(d)).astype(BF16)
            v_ref[h, :, sl] = jnp.where(low, swap(c), d).astype(BF16)
            a, b = (dq[n, h].astype(F32) for n in (2 * t, 2 * t + 1))
            q_ref[h, :half, sl] = jnp.where(lh, a, swap(b)).astype(BF16)
            q_ref[h, half:, sl] = jnp.where(lh, swap(a), b).astype(BF16)


def call(kernel, outs, *args, scratch=(), scalars=0, name):
    smem, vmem = pl.BlockSpec(memory_space=pltpu.SMEM), pl.BlockSpec(memory_space=pltpu.VMEM)
    return pl.pallas_call(
        kernel,
        out_shape=outs,
        in_specs=[smem] * scalars + [vmem] * (len(args) - scalars),
        out_specs=jax.tree.map(lambda _: vmem, outs),
        scratch_shapes=scratch,
        compiler_params=pltpu.CompilerParams(vmem_limit_bytes=40 * 1024 * 1024),
        name=name,
    )(*args)


def shape(*dims):
    return jax.ShapeDtypeStruct(dims, BF16)


def exchange(a, axes):
    return lax.all_to_all(a, axes, 0, 0, tiled=True)


def along_x(a, by):
    heads = lax.axis_size("x")
    return lax.ppermute(a, "x", [(i, (i + by) % heads) for i in range(heads)])


def per_device(query_rows, key_rows, value_rows, out_grad, out_weight, adjacency):
    parts = lax.axis_size("zh")
    heads, hours = lax.axis_size("x"), lax.axis_size("c")
    port_count = lax.axis_size(PORT_AXES)
    tm_count = lax.axis_size(TM_AXES)
    ports, _, width = query_rows.shape
    model = out_grad.shape[2]
    total = port_count * ports
    x, core = lax.axis_index("x"), lax.axis_index("c")
    q, k, v, g = (a.transpose(1, 0, 2) for a in (query_rows, key_rows, value_rows, out_grad))
    kv_send = call(pack_kv_kernel, shape(heads, parts, hours, ports, LANES), k, v, name="pack_kv")
    kv_got = exchange(kv_send.reshape(port_count, ports, LANES), PORT_AXES)
    adj = jnp.pad(adjacency, ((0, 0), (HEAD_DIM, LANES - HEAD_DIM - adjacency.shape[1])))
    qg = call(pack_qg_kernel, shape(hours, ports, heads * LANES + model), q, g, adj, name="pack_qg")
    qg = lax.all_gather(qg, "c")
    routed = call(
        route_kernel,
        (shape(hours, ports, LANES + model),) * heads,
        jnp.stack([x, core]),
        qg,
        scalars=1,
        name="route",
    )
    routed = [a if s == 0 else along_x(a, s) for s, a in enumerate(routed)]
    w_n = lax.dynamic_slice_in_dim(out_weight, x * HEAD_DIM, HEAD_DIM, 0)
    tiles = HEAD_DIM * model // (8 * LANES)
    chunk = ports + 8
    vec, acc = pltpu.VMEM((total, LANES), BF16), pltpu.VMEM((HEAD_DIM, total), F32)
    back, dq, dw = call(
        attend_kernel,
        (shape(port_count, chunk, LANES), shape(hours, heads, ports // 2, LANES), shape(tiles, 8, LANES)),
        kv_got,
        *(routed[s] for s in (0, 2, 1, 3)),
        w_n,
        scratch=[vec, vec, acc, acc],
        name="attend",
    )
    dw = exchange(dw, TM_AXES)
    dw = jnp.sum(dw.astype(F32), axis=0).astype(BF16)
    dq = lax.dynamic_index_in_dim(lax.all_gather(dq, "c"), core, 1, keepdims=False)
    dq = [dq[:, s] if s == 0 else along_x(dq[:, s], heads - s) for s in range(heads)]
    back = back.at[:, chunk - 8 :, :].set(jnp.broadcast_to(dw, (port_count, 8, LANES)))
    back, dq = lax.optimization_barrier((exchange(back, PORT_AXES), dq))
    back = back.reshape(heads, parts, hours, chunk, LANES)
    dw = back[:, :, :, chunk - 8 :, :].astype(F32)
    dw = (jnp.sum(dw, axis=(1, 2)) * (1.0 / (hours * tm_count))).astype(BF16)
    dw = exchange(jnp.broadcast_to(dw, (tm_count, *dw.shape)), TM_AXES)
    dw = dw.transpose(1, 0, 2, 3).reshape(heads, HEAD_DIM // 8, model // LANES, 8, LANES)
    dw = dw.transpose(0, 1, 3, 2, 4).reshape(width, model).astype(F32)
    grads = call(
        unpack_kernel,
        (shape(hours, ports, width),) * 3,
        x.reshape(1),
        back,
        *dq,
        scratch=[pltpu.VMEM((heads, hours, ports // 2, LANES), BF16)],
        scalars=1,
        name="unpack",
    )
    return *(a.transpose(1, 0, 2) for a in grads), dw


def solution(mesh):
    fine = Mesh(mesh.devices.reshape(4, 3, 2, 8, 4), PORT_AXES + TM_AXES)
    rows = P(PORT_AXES, TM_AXES, None)
    return jax.shard_map(
        per_device,
        mesh=fine,
        in_specs=(rows, rows, rows, rows, P(), P(PORT_AXES, None)),
        out_specs=(rows, rows, rows, P()),
        check_vma=False,
    )
```

```python
import jax
import jax.numpy as jnp
from jax import lax
from jax.experimental import pallas as pl
from jax.experimental.pallas import tpu as pltpu
from jax.sharding import Mesh, PartitionSpec as P

HEAD_DIM = 64
BLK = 32
LANES = 128
LOG2E = 1.4426950408889634
BIG = 1e30
F32, BF16 = jnp.float32, jnp.bfloat16

PORT_AXES = ("x", "zh", "c")
TM_AXES = ("y", "zl")
NT = (((1,), (1,)), ((), ()))
NN = (((1,), (0,)), ((), ()))
TN = (((0,), (0,)), ((), ()))


def dot(a, b, dims):
    return lax.dot_general(a, b, dims, preferred_element_type=F32)


def low_half(rows):
    return lax.broadcasted_iota(jnp.int32, (rows, LANES), 1) < HEAD_DIM


def swap(a):
    return jnp.concatenate([a[:, HEAD_DIM:], a[:, :HEAD_DIM]], axis=1)


def pack_kv_kernel(k_ref, v_ref, out_ref):
    hours, ports, width = k_ref.shape
    low = low_half(ports)
    for h in range(hours):
        for t in range(width // LANES):
            cols = slice(t * LANES, (t + 1) * LANES)
            k, v = k_ref[h, :, cols].astype(F32), v_ref[h, :, cols].astype(F32)
            even = jnp.where(low, k, swap(v)).astype(BF16)
            odd = jnp.where(low, swap(k), v).astype(BF16)
            for z in range(out_ref.shape[1]):
                out_ref[2 * t, z, h] = even
                out_ref[2 * t + 1, z, h] = odd


def pack_qg_kernel(q_ref, g_ref, adj_ref, out_ref):
    hours, ports, width = q_ref.shape
    low = low_half(ports)
    bias = (adj_ref[...].astype(F32) - 1.0) * BIG
    bias = jnp.concatenate(
        [jnp.broadcast_to(bias[b : b + 1, :], (BLK, LANES)) for b in range(ports // BLK)], axis=0
    )
    for h in range(hours):
        for t in range(width // LANES):
            q = q_ref[h, :, t * LANES : (t + 1) * LANES].astype(F32)
            at = 2 * t * LANES
            out_ref[h, :, at : at + LANES] = jnp.where(low, q, bias).astype(BF16)
            out_ref[h, :, at + LANES : at + 2 * LANES] = jnp.where(low, swap(q), bias).astype(BF16)
        out_ref[h, :, 2 * width :] = g_ref[h]


def route_kernel(at_ref, qg_ref, *out_refs):
    heads = len(out_refs)
    hour = at_ref[1]
    for s, out_ref in enumerate(out_refs):
        n = lax.rem(at_ref[0] + s, heads)
        for c in range(qg_ref.shape[0]):
            out_ref[c, :, :LANES] = qg_ref[c, hour, :, pl.ds(pl.multiple_of(n * LANES, LANES), LANES)]
            out_ref[c, :, LANES:] = qg_ref[c, hour, :, heads * LANES :]


def softmax_rows(qx, kx):
    s = dot(qx, kx, NT)
    top = jnp.max(s, axis=1, keepdims=True)
    e = jnp.exp2((s - top) * (0.125 * LOG2E))
    return e * (1.0 / jnp.sum(e, axis=1, keepdims=True))


def weight_kernel(kv_ref, p0_ref, p2_ref, p1_ref, p3_ref, dw_ref, kx, kv):
    sources, ports, _ = kv_ref.shape
    total = sources * ports
    parts = (p0_ref, p1_ref, p2_ref, p3_ref)
    own = len(parts) * 2 * ports
    rows = 4 * ports
    part = kv_ref[...].reshape(total, LANES)
    lane = lax.broadcasted_iota(jnp.int32, (total, LANES), 1)
    block = lax.shift_right_logical(lax.broadcasted_iota(jnp.int32, (total, LANES), 0), 5)
    hot = jnp.where(lane - HEAD_DIM == block, 1.0, 0.0)
    kv[...] = part
    kx[...] = jnp.where(lane < HEAD_DIM, part.astype(F32), hot).astype(BF16)
    dw = None
    for b in range(own // rows):
        mine = jnp.concatenate([parts[2 * b][...], parts[2 * b + 1][...]], axis=0)
        qx = mine[:, :, :LANES].reshape(rows, LANES)
        g = mine[:, :, LANES:].reshape(rows, -1)
        att = dot(softmax_rows(qx, kx[...]).astype(BF16), kv[...], NN).astype(BF16)
        part = dot(att, g, TN)
        dw = part if dw is None else dw + part
    dw = dw[HEAD_DIM:].astype(BF16)
    wide = dw.shape[1] // LANES
    for r in range(HEAD_DIM // 8):
        for c in range(wide):
            dw_ref[r * wide + c] = dw[r * 8 : (r + 1) * 8, c * LANES : (c + 1) * LANES]


def attend_kernel(kv_ref, p0_ref, p2_ref, p1_ref, p3_ref, w_ref, out_ref, dq_ref, kx, kv, dkt, dvt):
    sources, ports, _ = kv_ref.shape
    total = sources * ports
    parts = (p0_ref, p1_ref, p2_ref, p3_ref)
    own = len(parts) * 2 * ports
    rows = 4 * ports
    part = kv_ref[...].reshape(total, LANES)
    lane = lax.broadcasted_iota(jnp.int32, (total, LANES), 1)
    block = lax.shift_right_logical(lax.broadcasted_iota(jnp.int32, (total, LANES), 0), 5)
    hot = jnp.where(lane - HEAD_DIM == block, 1.0, 0.0)
    kv[...] = part
    kx[...] = jnp.where(lane < HEAD_DIM, part.astype(F32), hot).astype(BF16)
    w_n = jnp.concatenate([jnp.zeros_like(w_ref), w_ref[...]], axis=0)
    low = low_half(rows)
    per = rows // ports
    for b in range(own // rows):
        mine = jnp.concatenate([parts[2 * b][...], parts[2 * b + 1][...]], axis=0)
        qx = mine[:, :, :LANES].reshape(rows, LANES)
        g = mine[:, :, LANES:].reshape(rows, -1)
        d = dot(g, w_n, NT).astype(BF16)
        p = softmax_rows(qx, kx[...])
        p_low = p.astype(BF16)
        att = dot(p_low, kv[...], NN).astype(BF16)
        d32 = d.astype(F32)
        term = jnp.sum(d32 * att.astype(F32), axis=1, keepdims=True)
        dp = dot(d, kv[...], NT)
        ds = (p * (dp - term)).astype(BF16)
        dq = dot(ds, kv[...], NN) * 0.125
        qdt = jnp.where(low, qx.astype(F32), d32).T.astype(BF16)
        dk_part = dot(qdt[:HEAD_DIM], ds, NN)
        dv_part = dot(qdt[HEAD_DIM:], p_low, NN)
        if b:
            dkt[...] += dk_part
            dvt[...] += dv_part
        else:
            dkt[...] = dk_part
            dvt[...] = dv_part
        half = ports // 2
        for i in range(per):
            a, c = dq[i * ports : i * ports + half], dq[i * ports + half : (i + 1) * ports]
            dq_ref[i % 2, (b * per + i) // 2] = jnp.where(low_half(half), a, swap(c)).astype(BF16)
    both = jnp.concatenate([dkt[...] * 0.125, dvt[...]], axis=0).T.astype(BF16)
    for i in range(sources):
        out_ref[i, :ports, :] = both[i * ports : (i + 1) * ports]
        out_ref[i, ports:, :] = jnp.zeros((8, LANES), BF16)


def unpack_kernel(x_ref, t_ref, d0_ref, d1_ref, d2_ref, d3_ref, q_ref, k_ref, v_ref, dq):
    hours, ports, width = q_ref.shape
    low = low_half(ports)
    half = ports // 2
    lh = low_half(half)
    for s, ref in enumerate((d0_ref, d1_ref, d2_ref, d3_ref)):
        dq[lax.rem(x_ref[0] + s, 4)] = ref[...]
    for h in range(hours):
        for t in range(width // LANES):
            sl = slice(t * LANES, (t + 1) * LANES)
            c, d = (
                sum(t_ref[n, z, h, :ports].astype(F32) for z in range(t_ref.shape[1])) for n in (2 * t, 2 * t + 1)
            )
            k_ref[h, :, sl] = jnp.where(low, c, swap(d)).astype(BF16)
            v_ref[h, :, sl] = jnp.where(low, swap(c), d).astype(BF16)
            a, b = (dq[n, h].astype(F32) for n in (2 * t, 2 * t + 1))
            q_ref[h, :half, sl] = jnp.where(lh, a, swap(b)).astype(BF16)
            q_ref[h, half:, sl] = jnp.where(lh, swap(a), b).astype(BF16)


def call(kernel, outs, *args, scratch=(), scalars=0, name):
    smem, vmem = pl.BlockSpec(memory_space=pltpu.SMEM), pl.BlockSpec(memory_space=pltpu.VMEM)
    return pl.pallas_call(
        kernel,
        out_shape=outs,
        in_specs=[smem] * scalars + [vmem] * (len(args) - scalars),
        out_specs=jax.tree.map(lambda _: vmem, outs),
        scratch_shapes=scratch,
        compiler_params=pltpu.CompilerParams(vmem_limit_bytes=40 * 1024 * 1024),
        name=name,
    )(*args)


def shape(*dims):
    return jax.ShapeDtypeStruct(dims, BF16)


def exchange(a, axes):
    return lax.all_to_all(a, axes, 0, 0, tiled=True)


def along_x(a, by):
    heads = lax.axis_size("x")
    return lax.ppermute(a, "x", [(i, (i + by) % heads) for i in range(heads)])


def per_device(query_rows, key_rows, value_rows, out_grad, out_weight, adjacency):
    parts = lax.axis_size("zh")
    heads, hours = lax.axis_size("x"), lax.axis_size("c")
    port_count = lax.axis_size(PORT_AXES)
    tm_count = lax.axis_size(TM_AXES)
    ports, _, width = query_rows.shape
    model = out_grad.shape[2]
    total = port_count * ports
    x, core = lax.axis_index("x"), lax.axis_index("c")
    q, k, v, g = (a.transpose(1, 0, 2) for a in (query_rows, key_rows, value_rows, out_grad))
    kv_send = call(pack_kv_kernel, shape(heads, parts, hours, ports, LANES), k, v, name="pack_kv")
    kv_got = exchange(kv_send.reshape(port_count, ports, LANES), PORT_AXES)
    adj = jnp.pad(adjacency, ((0, 0), (HEAD_DIM, LANES - HEAD_DIM - adjacency.shape[1])))
    qg = call(pack_qg_kernel, shape(hours, ports, heads * LANES + model), q, g, adj, name="pack_qg")
    qg = lax.all_gather(qg, "c")
    routed = call(
        route_kernel,
        (shape(hours, ports, LANES + model),) * heads,
        jnp.stack([x, core]),
        qg,
        scalars=1,
        name="route",
    )
    routed = [a if s == 0 else along_x(a, s) for s, a in enumerate(routed)]
    w_n = lax.dynamic_slice_in_dim(out_weight, x * HEAD_DIM, HEAD_DIM, 0)
    tiles = HEAD_DIM * model // (8 * LANES)
    chunk = ports + 8
    vec, acc = pltpu.VMEM((total, LANES), BF16), pltpu.VMEM((HEAD_DIM, total), F32)
    shared = (kv_got, *(routed[s] for s in (0, 2, 1, 3)))
    dw = call(weight_kernel, shape(tiles, 8, LANES), *shared, scratch=[vec, vec], name="weight_rows")
    back, dq = call(
        attend_kernel,
        (shape(port_count, chunk, LANES), shape(hours, heads, ports // 2, LANES)),
        *shared,
        w_n,
        scratch=[vec, vec, acc, acc],
        name="attend",
    )
    dw = exchange(dw, TM_AXES)
    dw = jnp.sum(dw.astype(F32), axis=0).astype(BF16)
    dq = lax.dynamic_index_in_dim(lax.all_gather(dq, "c"), core, 1, keepdims=False)
    dq = [dq[:, s] if s == 0 else along_x(dq[:, s], heads - s) for s in range(heads)]
    back = back.at[:, chunk - 8 :, :].set(jnp.broadcast_to(dw, (port_count, 8, LANES)))
    back, dq = lax.optimization_barrier((exchange(back, PORT_AXES), dq))
    back = back.reshape(heads, parts, hours, chunk, LANES)
    dw = back[:, :, :, chunk - 8 :, :].astype(F32)
    dw = (jnp.sum(dw, axis=(1, 2)) * (1.0 / (hours * tm_count))).astype(BF16)
    dw = exchange(jnp.broadcast_to(dw, (tm_count, *dw.shape)), TM_AXES)
    dw = dw.transpose(1, 0, 2, 3).reshape(heads, HEAD_DIM // 8, model // LANES, 8, LANES)
    dw = dw.transpose(0, 1, 3, 2, 4).reshape(width, model).astype(F32)
    grads = call(
        unpack_kernel,
        (shape(hours, ports, width),) * 3,
        x.reshape(1),
        back,
        *dq,
        scratch=[pltpu.VMEM((heads, hours, ports // 2, LANES), BF16)],
        scalars=1,
        name="unpack",
    )
    return *(a.transpose(1, 0, 2) for a in grads), dw


def solution(mesh):
    fine = Mesh(mesh.devices.reshape(4, 3, 2, 8, 4), PORT_AXES + TM_AXES)
    rows = P(PORT_AXES, TM_AXES, None)
    return jax.shard_map(
        per_device,
        mesh=fine,
        in_specs=(rows, rows, rows, rows, P(), P(PORT_AXES, None)),
        out_specs=(rows, rows, rows, P()),
        check_vma=False,
    )
```

```python
import jax
import jax.numpy as jnp
from jax import lax
from jax.experimental import pallas as pl
from jax.experimental.pallas import tpu as pltpu
from jax.sharding import Mesh, PartitionSpec as P

HEAD_DIM = 64
BLK = 32
LANES = 128
LOG2E = 1.4426950408889634
BIG = 1e30
F32, BF16 = jnp.float32, jnp.bfloat16

PORT_AXES = ("x", "zh", "c")
TM_AXES = ("y", "zl")
NT = (((1,), (1,)), ((), ()))
NN = (((1,), (0,)), ((), ()))
TN = (((0,), (0,)), ((), ()))


def dot(a, b, dims):
    return lax.dot_general(a, b, dims, preferred_element_type=F32)


def low_half(rows):
    return lax.broadcasted_iota(jnp.int32, (rows, LANES), 1) < HEAD_DIM


def swap(a):
    return jnp.concatenate([a[:, HEAD_DIM:], a[:, :HEAD_DIM]], axis=1)


def pack_kv_kernel(k_ref, v_ref, out_ref):
    hours, ports, width = k_ref.shape
    low = low_half(ports)
    for h in range(hours):
        for t in range(width // LANES):
            cols = slice(t * LANES, (t + 1) * LANES)
            k, v = k_ref[h, :, cols].astype(F32), v_ref[h, :, cols].astype(F32)
            even = jnp.where(low, k, swap(v)).astype(BF16)
            odd = jnp.where(low, swap(k), v).astype(BF16)
            for z in range(out_ref.shape[1]):
                out_ref[2 * t, z, h] = even
                out_ref[2 * t + 1, z, h] = odd


def pack_qg_kernel(q_ref, g_ref, adj_ref, out_ref):
    hours, ports, width = q_ref.shape
    low = low_half(ports)
    bias = (adj_ref[...].astype(F32) - 1.0) * BIG
    bias = jnp.concatenate(
        [jnp.broadcast_to(bias[b : b + 1, :], (BLK, LANES)) for b in range(ports // BLK)], axis=0
    )
    for h in range(hours):
        for t in range(width // LANES):
            q = q_ref[h, :, t * LANES : (t + 1) * LANES].astype(F32)
            at = 2 * t * LANES
            out_ref[h, :, at : at + LANES] = jnp.where(low, q, bias).astype(BF16)
            out_ref[h, :, at + LANES : at + 2 * LANES] = jnp.where(low, swap(q), bias).astype(BF16)
        out_ref[h, :, 2 * width :] = g_ref[h]


def route_kernel(at_ref, qg_ref, *out_refs):
    heads = len(out_refs)
    hour = at_ref[1]
    for s, out_ref in enumerate(out_refs):
        n = lax.rem(at_ref[0] + s, heads)
        for c in range(qg_ref.shape[0]):
            out_ref[c, :, :LANES] = qg_ref[c, hour, :, pl.ds(pl.multiple_of(n * LANES, LANES), LANES)]
            out_ref[c, :, LANES:] = qg_ref[c, hour, :, heads * LANES :]


def softmax_rows(qx, kx):
    s = dot(qx, kx, NT)
    top = jnp.max(s, axis=1, keepdims=True)
    e = jnp.exp2((s - top) * (0.125 * LOG2E))
    return e * (1.0 / jnp.sum(e, axis=1, keepdims=True))


def weight_kernel(kv_ref, p0_ref, p2_ref, p1_ref, p3_ref, dw_ref, kx, kv):
    sources, ports, _ = kv_ref.shape
    total = sources * ports
    parts = (p0_ref, p1_ref, p2_ref, p3_ref)
    own = len(parts) * 2 * ports
    rows = 4 * ports
    part = kv_ref[...].reshape(total, LANES)
    lane = lax.broadcasted_iota(jnp.int32, (total, LANES), 1)
    block = lax.shift_right_logical(lax.broadcasted_iota(jnp.int32, (total, LANES), 0), 5)
    hot = jnp.where(lane - HEAD_DIM == block, 1.0, 0.0)
    kv[...] = jnp.where(lane < HEAD_DIM, 1.0, part.astype(F32)).astype(BF16)
    kx[...] = jnp.where(lane < HEAD_DIM, part.astype(F32), hot).astype(BF16)
    dw = None
    for b in range(own // rows):
        mine = jnp.concatenate([parts[2 * b][...], parts[2 * b + 1][...]], axis=0)
        qx = mine[:, :, :LANES].reshape(rows, LANES)
        g = mine[:, :, LANES:].reshape(rows, -1)
        s = dot(qx, kx[...], NT)
        top = jnp.max(s, axis=1, keepdims=True)
        e = jnp.exp2((s - top) * (0.125 * LOG2E)).astype(BF16)
        att = dot(e, kv[...], NN)
        att = (att * (1.0 / att[:, :1])).astype(BF16)
        part = dot(att, g, TN)
        dw = part if dw is None else dw + part
    dw = dw[HEAD_DIM:].astype(BF16)
    wide = dw.shape[1] // LANES
    for r in range(HEAD_DIM // 8):
        for c in range(wide):
            dw_ref[r * wide + c] = dw[r * 8 : (r + 1) * 8, c * LANES : (c + 1) * LANES]


def attend_kernel(kv_ref, p0_ref, p2_ref, p1_ref, p3_ref, w_ref, out_ref, dq_ref, kx, kv, dkt, dvt):
    sources, ports, _ = kv_ref.shape
    total = sources * ports
    parts = (p0_ref, p1_ref, p2_ref, p3_ref)
    own = len(parts) * 2 * ports
    rows = 4 * ports
    part = kv_ref[...].reshape(total, LANES)
    lane = lax.broadcasted_iota(jnp.int32, (total, LANES), 1)
    block = lax.shift_right_logical(lax.broadcasted_iota(jnp.int32, (total, LANES), 0), 5)
    hot = jnp.where(lane - HEAD_DIM == block, 1.0, 0.0)
    kv[...] = part
    kx[...] = jnp.where(lane < HEAD_DIM, part.astype(F32), hot).astype(BF16)
    w_n = jnp.concatenate([jnp.zeros_like(w_ref), w_ref[...]], axis=0)
    low = low_half(rows)
    per = rows // ports
    for b in range(own // rows):
        mine = jnp.concatenate([parts[2 * b][...], parts[2 * b + 1][...]], axis=0)
        qx = mine[:, :, :LANES].reshape(rows, LANES)
        g = mine[:, :, LANES:].reshape(rows, -1)
        d = dot(g, w_n, NT).astype(BF16)
        p = softmax_rows(qx, kx[...])
        p_low = p.astype(BF16)
        att = dot(p_low, kv[...], NN).astype(BF16)
        d32 = d.astype(F32)
        term = jnp.sum(d32 * att.astype(F32), axis=1, keepdims=True)
        dp = dot(d, kv[...], NT)
        ds = (p * (dp - term)).astype(BF16)
        dq = dot(ds, kv[...], NN) * 0.125
        qdt = jnp.where(low, qx.astype(F32), d32).T.astype(BF16)
        dk_part = dot(qdt[:HEAD_DIM], ds, NN)
        dv_part = dot(qdt[HEAD_DIM:], p_low, NN)
        if b:
            dkt[...] += dk_part
            dvt[...] += dv_part
        else:
            dkt[...] = dk_part
            dvt[...] = dv_part
        half = ports // 2
        for i in range(per):
            a, c = dq[i * ports : i * ports + half], dq[i * ports + half : (i + 1) * ports]
            dq_ref[i % 2, (b * per + i) // 2] = jnp.where(low_half(half), a, swap(c)).astype(BF16)
    both = jnp.concatenate([dkt[...] * 0.125, dvt[...]], axis=0).T.astype(BF16)
    for i in range(sources):
        out_ref[i, :ports, :] = both[i * ports : (i + 1) * ports]
        out_ref[i, ports:, :] = jnp.zeros((8, LANES), BF16)


def unpack_kernel(x_ref, t_ref, d0_ref, d1_ref, d2_ref, d3_ref, q_ref, k_ref, v_ref, dq):
    hours, ports, width = q_ref.shape
    low = low_half(ports)
    half = ports // 2
    lh = low_half(half)
    for s, ref in enumerate((d0_ref, d1_ref, d2_ref, d3_ref)):
        dq[lax.rem(x_ref[0] + s, 4)] = ref[...]
    for h in range(hours):
        for t in range(width // LANES):
            sl = slice(t * LANES, (t + 1) * LANES)
            c, d = (
                sum(t_ref[n, z, h, :ports].astype(F32) for z in range(t_ref.shape[1])) for n in (2 * t, 2 * t + 1)
            )
            k_ref[h, :, sl] = jnp.where(low, c, swap(d)).astype(BF16)
            v_ref[h, :, sl] = jnp.where(low, swap(c), d).astype(BF16)
            a, b = (dq[n, h].astype(F32) for n in (2 * t, 2 * t + 1))
            q_ref[h, :half, sl] = jnp.where(lh, a, swap(b)).astype(BF16)
            q_ref[h, half:, sl] = jnp.where(lh, swap(a), b).astype(BF16)


def call(kernel, outs, *args, scratch=(), scalars=0, name):
    smem, vmem = pl.BlockSpec(memory_space=pltpu.SMEM), pl.BlockSpec(memory_space=pltpu.VMEM)
    return pl.pallas_call(
        kernel,
        out_shape=outs,
        in_specs=[smem] * scalars + [vmem] * (len(args) - scalars),
        out_specs=jax.tree.map(lambda _: vmem, outs),
        scratch_shapes=scratch,
        compiler_params=pltpu.CompilerParams(vmem_limit_bytes=40 * 1024 * 1024),
        name=name,
    )(*args)


def shape(*dims):
    return jax.ShapeDtypeStruct(dims, BF16)


def exchange(a, axes):
    return lax.all_to_all(a, axes, 0, 0, tiled=True)


def along_x(a, by):
    heads = lax.axis_size("x")
    return lax.ppermute(a, "x", [(i, (i + by) % heads) for i in range(heads)])


def per_device(query_rows, key_rows, value_rows, out_grad, out_weight, adjacency):
    parts = lax.axis_size("zh")
    heads, hours = lax.axis_size("x"), lax.axis_size("c")
    port_count = lax.axis_size(PORT_AXES)
    tm_count = lax.axis_size(TM_AXES)
    ports, _, width = query_rows.shape
    model = out_grad.shape[2]
    total = port_count * ports
    x, core = lax.axis_index("x"), lax.axis_index("c")
    q, k, v, g = (a.transpose(1, 0, 2) for a in (query_rows, key_rows, value_rows, out_grad))
    kv_send = call(pack_kv_kernel, shape(heads, parts, hours, ports, LANES), k, v, name="pack_kv")
    kv_got = exchange(kv_send.reshape(port_count, ports, LANES), PORT_AXES)
    adj = jnp.pad(adjacency, ((0, 0), (HEAD_DIM, LANES - HEAD_DIM - adjacency.shape[1])))
    qg = call(pack_qg_kernel, shape(hours, ports, heads * LANES + model), q, g, adj, name="pack_qg")
    qg = lax.all_gather(qg, "c")
    routed = call(
        route_kernel,
        (shape(hours, ports, LANES + model),) * heads,
        jnp.stack([x, core]),
        qg,
        scalars=1,
        name="route",
    )
    routed = [a if s == 0 else along_x(a, s) for s, a in enumerate(routed)]
    w_n = lax.dynamic_slice_in_dim(out_weight, x * HEAD_DIM, HEAD_DIM, 0)
    tiles = HEAD_DIM * model // (8 * LANES)
    chunk = ports + 8
    vec, acc = pltpu.VMEM((total, LANES), BF16), pltpu.VMEM((HEAD_DIM, total), F32)
    shared = (kv_got, *(routed[s] for s in (0, 2, 1, 3)))
    dw = call(weight_kernel, shape(tiles, 8, LANES), *shared, scratch=[vec, vec], name="weight_rows")
    back, dq = call(
        attend_kernel,
        (shape(port_count, chunk, LANES), shape(hours, heads, ports // 2, LANES)),
        *shared,
        w_n,
        scratch=[vec, vec, acc, acc],
        name="attend",
    )
    dw = exchange(dw, TM_AXES)
    dw = jnp.sum(dw.astype(F32), axis=0).astype(BF16)
    dq = lax.dynamic_index_in_dim(lax.all_gather(dq, "c"), core, 1, keepdims=False)
    dq = [dq[:, s] if s == 0 else along_x(dq[:, s], heads - s) for s in range(heads)]
    back = back.at[:, chunk - 8 :, :].set(jnp.broadcast_to(dw, (port_count, 8, LANES)))
    back, dq = lax.optimization_barrier((exchange(back, PORT_AXES), dq))
    back = back.reshape(heads, parts, hours, chunk, LANES)
    dw = back[:, :, :, chunk - 8 :, :].astype(F32)
    dw = (jnp.sum(dw, axis=(1, 2)) * (1.0 / (hours * tm_count))).astype(BF16)
    dw = exchange(jnp.broadcast_to(dw, (tm_count, *dw.shape)), TM_AXES)
    dw = dw.transpose(1, 0, 2, 3).reshape(heads, HEAD_DIM // 8, model // LANES, 8, LANES)
    dw = dw.transpose(0, 1, 3, 2, 4).reshape(width, model).astype(F32)
    grads = call(
        unpack_kernel,
        (shape(hours, ports, width),) * 3,
        x.reshape(1),
        back,
        *dq,
        scratch=[pltpu.VMEM((heads, hours, ports // 2, LANES), BF16)],
        scalars=1,
        name="unpack",
    )
    return *(a.transpose(1, 0, 2) for a in grads), dw


def solution(mesh):
    fine = Mesh(mesh.devices.reshape(4, 3, 2, 8, 4), PORT_AXES + TM_AXES)
    rows = P(PORT_AXES, TM_AXES, None)
    return jax.shard_map(
        per_device,
        mesh=fine,
        in_specs=(rows, rows, rows, rows, P(), P(PORT_AXES, None)),
        out_specs=(rows, rows, rows, P()),
        check_vma=False,
    )
```
